256 devices in a mesh: seq: 32 (over x, z), head: 8 (over y, core).
Axes of the slice: x: 4, y: 4, z: 8, core: 2. Of those that a mesh axis runs over, the one named last changes fastest.
Arguments:
- values: bfloat16 [24, 64, 131072], P('head', None, 'seq'), may hold values from -6 to 6
- b_rows: bfloat16 [128, 131072], P(None, ('seq', 'head')), may hold values from -0.59765625 to 0.59765625
- c_rows: bfloat16 [128, 131072], P(None, ('seq', 'head')), may hold values from -0.59765625 to 0.59765625
- log_decay: float32 [24, 131072], P('head', 'seq'), may hold values from -0.6 to 0
- level_weight: float32 [12, 24, 131072], P(None, 'head', 'seq'), may hold values from 0 to 2
Outputs:
- layer_out: bfloat16 [24, 64, 131072], P('head', None, 'seq')
The draws below stay inside these ranges and needn't reach their ends.
All inputs are finite; a program needn't handle non-finite values.
Results may differ from the reference program's by a relative error of at most 0.0034.
Values may be sent and summed in bfloat16 or wider, within the bound.
No kernel may reach another device: no remote copies, remote signals or barrier semaphores. Data moves between devices by JAX's collectives and lax.ppermute only.
A program may use at most 128 MiB of HBM per device.

```python
import math
import jax
import jax.numpy as jnp
from jax import lax

HEAD_TOTAL = 24
STATE = 128
HEAD_DIM = 64
STRETCH = 64
TOKEN_TOTAL = 131072
LEVELS = 12


def draw_log_decay(key, part):
    key = jax.random.fold_in(key, 11)
    key_sequence = jax.random.split(key, 6)
    slow_share = 0.5
    slow_mask = jax.random.bernoulli(key_sequence[0], slow_share, (HEAD_TOTAL, 1))
    slow_rate = 0.25 * math.log(10.0) / TOKEN_TOTAL
    fast_rate = jnp.exp(jax.random.uniform(key_sequence[1], (HEAD_TOTAL, 1), jnp.float32, math.log(1.0 / 50.0), math.log(1.0 / 30.0)))
    baseline_rate = jnp.where(slow_mask, slow_rate, fast_rate)
    block_multiplier = jnp.repeat(jax.random.uniform(key_sequence[2], (HEAD_TOTAL, TOKEN_TOTAL // STRETCH), jnp.float32, 0.5, 1.5), STRETCH, axis=1)
    jaggedness = jax.random.uniform(key_sequence[3], (HEAD_TOTAL, TOKEN_TOTAL), jnp.float32, 0.4, 1.6)
    spike_mask = jax.random.bernoulli(key_sequence[4], 3.0 / TOKEN_TOTAL, (HEAD_TOTAL, TOKEN_TOTAL))
    spike_length = jax.random.uniform(key_sequence[5], (HEAD_TOTAL, TOKEN_TOTAL), jnp.float32, 0.22, 0.5)
    return -(baseline_rate * block_multiplier * jaggedness + jnp.where(spike_mask, spike_length, 0.0))


def draw_level_weight(key, part):
    key = jax.random.fold_in(key, 23)
    base_draw = jnp.exp(jax.random.uniform(key, (LEVELS, HEAD_TOTAL, TOKEN_TOTAL), jnp.float32, math.log(0.5), math.log(2.0)))
    level_ids = jnp.arange(LEVELS).astype(jnp.float32)
    level_scale = jnp.exp2(-0.5 * jnp.maximum(level_ids - 1.0, 0.0))
    return level_scale[:, None, None] * base_draw


def block_levels(key, extent, pieces, low, largest):
    def one(axis_at, parts):
        heights = jax.random.uniform(jax.random.fold_in(jax.random.fold_in(key, 6), axis_at), (parts,), jnp.float32, low / len(pieces), largest / len(pieces))
        return jnp.repeat(jnp.exp(heights), extent[axis_at] // parts).reshape((-1,) + (1,) * (len(extent) - axis_at - 1))

    gain = one(*pieces[0])
    for cut in pieces[1:]:
        gain = gain * one(*cut)
    return gain


def gaussian(stream_key, dims, deviation, most, cuts=(), dtype=jnp.bfloat16):
    factor_of = block_levels(stream_key, dims, cuts, -0.22, 0.18) if cuts else 1.0
    values = jax.random.normal(stream_key, dims, jnp.float32) * deviation * factor_of
    return jnp.minimum(jnp.maximum(values, -most), most).astype(dtype)


def setup_inputs(seed: int = 0) -> dict:
    arg_keys = jax.random.split(jax.random.key(seed), 6)
    values = gaussian(arg_keys[0], (HEAD_TOTAL, HEAD_DIM, TOKEN_TOTAL), 1.0, 6.0, ((0, 8), (2, 32)))
    b_rows = gaussian(arg_keys[1], (STATE, TOKEN_TOTAL), 0.1, 0.59765625, ((1, 256),))
    c_rows = gaussian(arg_keys[2], (STATE, TOKEN_TOTAL), 0.1, 0.59765625, ((1, 256),))
    log_decay = draw_log_decay(jax.random.fold_in(arg_keys[5], 71), 0)
    level_weight = draw_level_weight(jax.random.fold_in(arg_keys[5], 71), 0)
    return {"values": values, "b_rows": b_rows, "c_rows": c_rows, "log_decay": log_decay, "level_weight": level_weight}


def reference(values, b_rows, c_rows, log_decay, level_weight):
    stretch_count = TOKEN_TOTAL // STRETCH
    b_blk = b_rows.astype(jnp.float32).reshape(STATE, stretch_count, STRETCH)
    c_blk = c_rows.astype(jnp.float32).reshape(STATE, stretch_count, STRETCH)
    scores = jnp.einsum('nkt,nks->kts', c_blk, b_blk, precision=lax.Precision.HIGHEST)
    causal = jnp.arange(STRETCH)[:, None] >= jnp.arange(STRETCH)[None, :]
    weights_t = jnp.transpose(level_weight, (1, 0, 2))

    def one_head(packed):
        head_vals, head_decay, head_weight = packed
        val_blk = head_vals.astype(jnp.float32).reshape(HEAD_DIM, stretch_count, STRETCH)
        cum_log = jnp.cumsum(head_decay.reshape(stretch_count, STRETCH), axis=1)
        stretch_tot = cum_log[:, -1]
        diff_log = cum_log[:, :, None] - cum_log[:, None, :]
        decay = jnp.exp(jnp.where(causal[None], diff_log, -jnp.inf))
        weight_zero = head_weight[0].reshape(stretch_count, STRETCH)
        mix = (weight_zero[:, :, None] * decay * scores).astype(jnp.bfloat16)
        result = jnp.einsum('kts,pks->pkt', mix.astype(jnp.float32), val_blk, precision=lax.Precision.HIGHEST)
        keys_decayed = (jnp.exp(stretch_tot[:, None] - cum_log)[None] * b_blk).astype(jnp.bfloat16)
        state = jnp.einsum('nks,pks->knp', keys_decayed.astype(jnp.float32), val_blk, precision=lax.Precision.HIGHEST)
        c_exp = jnp.exp(cum_log)[None] * c_blk
        agg, tot_blk = state, stretch_tot
        for level in range(LEVELS - 1):
            span = 2 ** level
            groups = stretch_count // (2 * span)
            paired = agg.reshape(groups, 2, STATE, HEAD_DIM)
            left_part = paired[:, 0]
            right_part = paired[:, 1]
            tot_pair = tot_blk.reshape(groups, 2)
            src_tot = stretch_tot.reshape(groups, 2, span)[:, 1]
            pre_tot = jnp.concatenate([jnp.zeros((groups, 1), jnp.float32), jnp.cumsum(src_tot[:, :-1], axis=1)], axis=1)
            carried = jnp.exp(pre_tot)[:, :, None, None] * left_part[:, None]
            c_right = c_exp.reshape(STATE, groups, 2, span, STRETCH)[:, :, 1]
            w_right = head_weight[level + 1].reshape(groups, 2, span, STRETCH)[:, 1]
            contrib = jnp.einsum('ngwq,gwnp->pgwq', c_right, carried, precision=lax.Precision.HIGHEST) * w_right[None]
            result = result.reshape(HEAD_DIM, groups, 2, span, STRETCH).at[:, :, 1].add(contrib).reshape(HEAD_DIM, stretch_count, STRETCH)
            agg = jnp.exp(tot_pair[:, 1])[:, None, None] * left_part + right_part
            tot_blk = tot_pair[:, 0] + tot_pair[:, 1]
        return result.reshape(HEAD_DIM, TOKEN_TOTAL).astype(jnp.bfloat16)

    return lax.map(one_head, (values, log_decay, weights_t))
```

```python
import jax
import jax.numpy as jnp
from jax import lax
from jax.experimental import pallas as pl
from jax.experimental.pallas import tpu as pltpu
from jax.sharding import PartitionSpec as P

STRETCH = 64
HEADS = 3
WIDTH = 64
STATE = 128
ROWS = HEADS * WIDTH
PIECE = 512
PIECES = 8
TOKENS = PIECE * PIECES
LOCAL = 6
CROSS = 5
FIRST = (0, 32, 48, 56, 60, 62, 63)
F32 = jnp.float32
BF16 = jnp.bfloat16

VMEM = pl.BlockSpec(memory_space=pltpu.VMEM)
SMEM = pl.BlockSpec(memory_space=pltpu.SMEM)


def params():
    return pltpu.CompilerParams(vmem_limit_bytes=56 * 1024 * 1024)


def decay_kernel(ld_ref, lw_ref, sc_ref, binv_ref, dec_ref, grp_ref):
    tiles = TOKENS // 128
    lane = lax.broadcasted_iota(jnp.int32, (HEADS, 128), 1)
    local = lane & 63
    runs = []
    for i in range(tiles):
        cols = pl.ds(i * 128, 128)
        ld = ld_ref[:, cols]
        cum = ld
        for k in (1, 2, 4, 8, 16, 32):
            cum = cum + jnp.where(local >= k, pltpu.roll(cum, k, 1), 0.0)
        rest = ld
        for k in (1, 2, 4, 8, 16, 32):
            rest = rest + jnp.where(local < 64 - k, pltpu.roll(rest, 128 - k, 1), 0.0)
        runs.append(cum)
        grow = jnp.exp(cum)
        dec_ref[:, cols] = jnp.exp(rest - ld)
        binv_ref[:, cols] = jnp.exp(-cum)
        sc_ref[0, :, cols] = lw_ref[0, :, cols] * grow
        sc_ref[1, :, cols] = jnp.where(lane >= 64, lw_ref[1, :, cols] * grow, 0.0)
        grp_ref[:, cols] = jnp.broadcast_to(grow[:, 127:128], (HEADS, 128))
        left = jnp.broadcast_to(cum[:, 63:64], (HEADS, 128))
        runs[i] = cum + jnp.where(lane >= 64, left, 0.0)
    for level in range(2, LOCAL + 2):
        span = 2 ** (level - 2)
        ends = [jnp.broadcast_to(runs[i][:, 127:128], (HEADS, 128)) for i in range(span - 1, tiles, span)]
        for i in range(tiles):
            cols = pl.ds(i * 128, 128)
            if level <= LOCAL:
                if (i // span) % 2:
                    sc_ref[level, :, cols] = lw_ref[level, :, cols] * jnp.exp(runs[i])
                else:
                    sc_ref[level, :, cols] = jnp.zeros((HEADS, 128), F32)
            else:
                grow = jnp.exp(runs[i])
                for up in range(CROSS):
                    sc_ref[level + up, :, cols] = lw_ref[level + up, :, cols] * grow
        if level <= LOCAL:
            for i in range(tiles // (2 * span)):
                grp_ref[:, pl.ds((FIRST[level - 1] + i) * 128, 128)] = jnp.exp(ends[2 * i + 1])
            for i in range(tiles):
                if (i // span) % 2:
                    runs[i] = runs[i] + ends[i // span - 1]
        else:
            grp_ref[:, pl.ds(63 * 128, 128)] = ends[0]


def decay_rows(log_decay, level_weight):
    row = jax.ShapeDtypeStruct((HEADS, TOKENS), F32)
    return pl.pallas_call(
        decay_kernel,
        out_shape=[
            jax.ShapeDtypeStruct((1 + LOCAL + CROSS, HEADS, TOKENS), F32),
            row,
            row,
            jax.ShapeDtypeStruct((HEADS, 64 * 128), F32),
        ],
        in_specs=[VMEM] * 2,
        out_specs=[VMEM] * 4,
        compiler_params=params(),
        name="decay_rows",
    )(log_decay, level_weight)


def state_kernel(order_ref, v_ref, dec_ref, grp_ref, *refs):
    b_refs = refs[:PIECES]
    agg_ref, end_ref, b_buf, p_buf = refs[PIECES:]
    for q in range(PIECES):
        b_buf[q] = b_refs[q][...]
    lane = lax.broadcasted_iota(jnp.int32, (WIDTH, 128), 1)
    first = lane < 64

    def factor(h, slot):
        return grp_ref[h : h + 1, pl.ds(pl.multiple_of(slot * 128, 128), 128)]

    def piece(q, carry):
        j = order_ref[q]
        for h in range(HEADS):
            here = slice(h * WIDTH, (h + 1) * WIDTH)
            tops = []
            for a in range(4):
                cols = pl.ds(pl.multiple_of(j * PIECE + a * 128, 128), 128)
                b = b_buf[q, :, a * 128 : (a + 1) * 128].astype(F32)
                v = v_ref[h, :, cols]
                keys = (dec_ref[h : h + 1, cols] * b).astype(BF16)
                zero = jnp.zeros_like(v)
                both = jnp.concatenate([jnp.where(first, v, zero), jnp.where(first, zero, v)], axis=0)
                s = lax.dot_general(both, keys, (((1,), (1,)), ((), ())), preferred_element_type=F32)
                agg_ref[j * 4 + a, here, :] = s[:WIDTH].astype(BF16)
                tops.append(factor(h, j * 4 + a) * s[:WIDTH] + s[WIDTH:])
            agg_ref[FIRST[1] + j * 2, here, :] = tops[0].astype(BF16)
            agg_ref[FIRST[1] + j * 2 + 1, here, :] = tops[2].astype(BF16)
            lo = factor(h, FIRST[1] + j * 2) * tops[0] + tops[1]
            hi = factor(h, FIRST[1] + j * 2 + 1) * tops[2] + tops[3]
            agg_ref[FIRST[2] + j, here, :] = lo.astype(BF16)
            p_buf[j, here, :] = factor(h, FIRST[2] + j) * lo + hi
        return carry

    lax.fori_loop(0, PIECES, piece, 0)
    for h in range(HEADS):
        here = slice(h * WIDTH, (h + 1) * WIDTH)
        tops = [p_buf[j, here, :] for j in range(PIECES)]
        for level in range(4, LOCAL + 1):
            nxt = []
            for i in range(len(tops) // 2):
                slot = FIRST[level - 1] + i
                agg_ref[slot, here, :] = tops[2 * i].astype(BF16)
                nxt.append(factor(h, slot) * tops[2 * i] + tops[2 * i + 1])
            tops = nxt
        end_ref[here, :] = tops[0]
    end_ref[ROWS : ROWS + 8, :] = jnp.concatenate([grp_ref[:, 63 * 128 :], jnp.zeros((5, 128), F32)], axis=0)


def block_states(order, values, dec, grp, b_list):
    return pl.pallas_call(
        state_kernel,
        out_shape=[
            jax.ShapeDtypeStruct((63, ROWS, STATE), BF16),
            jax.ShapeDtypeStruct((ROWS + 8, STATE), F32),
        ],
        in_specs=[SMEM] + [VMEM] * (3 + PIECES),
        out_specs=[VMEM] * 2,
        scratch_shapes=[
            pltpu.VMEM((PIECES, STATE, PIECE), BF16),
            pltpu.VMEM((PIECES, ROWS, STATE), F32),
        ],
        compiler_params=params(),
        name="block_states",
    )(order, values, dec, grp, *b_list)


def local_kernel(order_ref, v_ref, sc_ref, binv_ref, agg_ref, *refs):
    b_refs = refs[:PIECES]
    c_refs = refs[PIECES : 2 * PIECES]
    out_ref, b_buf, c_buf = refs[2 * PIECES :]
    for q in range(PIECES):
        b_buf[q] = b_refs[q][...]
        c_buf[q] = c_refs[q][...]
    s_id = lax.broadcasted_iota(jnp.int32, (128, 128), 0)
    t_id = lax.broadcasted_iota(jnp.int32, (128, 128), 1)
    keep = (s_id <= t_id) & ((s_id >> 6) == (t_id >> 6))

    def piece(q, carry):
        j = order_ref[q]
        base = j * PIECE
        for a in range(4):
            cols = pl.ds(pl.multiple_of(base + a * 128, 128), 128)
            c = c_buf[q, :, a * 128 : (a + 1) * 128]
            b = b_buf[q, :, a * 128 : (a + 1) * 128]
            scores = lax.dot_general(b, c, (((0,), (0,)), ((), ())), preferred_element_type=F32)
            scores = jnp.where(keep, scores, 0.0)
            slots = [(1, j * 4 + a)]
            if a & 1:
                slots.append((2, FIRST[1] + j * 2 + a // 2))
            if a & 2:
                slots.append((3, FIRST[2] + j))
            reads = [(level, jnp.dot(agg_ref[slot], c, preferred_element_type=F32)) for level, slot in slots]
            for h in range(HEADS):
                here = slice(h * WIDTH, (h + 1) * WIDTH)
                col = jnp.transpose(jnp.broadcast_to(binv_ref[h : h + 1, cols], (128, 128)))
                mix = ((sc_ref[0, h : h + 1, cols] * scores) * col).astype(BF16)
                acc = jnp.dot(v_ref[h, :, cols], mix, preferred_element_type=F32)
                for level, r in reads:
                    acc = acc + sc_ref[level, h : h + 1, cols] * r[here, :]
                out_ref[h, :, cols] = acc
        for level in range(4, LOCAL + 1):
            bit = level - 4

            @pl.when(((j >> bit) & 1) == 1)
            def _():
                slot = FIRST[level - 1] + (j >> (bit + 1))
                for a in range(2):
                    cols = pl.ds(pl.multiple_of(base + a * 256, 256), 256)
                    c = c_buf[q, :, a * 256 : (a + 1) * 256]
                    r = jnp.dot(agg_ref[slot], c, preferred_element_type=F32)
                    for h in range(HEADS):
                        here = slice(h * WIDTH, (h + 1) * WIDTH)
                        out_ref[h, :, cols] += sc_ref[level, h : h + 1, cols] * r[here, :]

        return carry

    lax.fori_loop(0, PIECES, piece, 0)


def local_part(order, values, sc, binv, agg, b_list, c_list):
    return pl.pallas_call(
        local_kernel,
        out_shape=jax.ShapeDtypeStruct((HEADS, WIDTH, TOKENS), F32),
        in_specs=[SMEM] + [VMEM] * (4 + 2 * PIECES),
        out_specs=VMEM,
        scratch_shapes=[
            pltpu.VMEM((PIECES, STATE, PIECE), BF16),
            pltpu.VMEM((PIECES, STATE, PIECE), BF16),
        ],
        compiler_params=params(),
        name="local_part",
    )(order, values, sc, binv, agg, *b_list, *c_list)


def cross_kernel(order_ref, loc_ref, sc_ref, fac_ref, *refs):
    s_refs = refs[:CROSS]
    c_refs = refs[CROSS : CROSS + PIECES]
    out_ref, c_buf = refs[CROSS + PIECES :]
    for q in range(PIECES):
        c_buf[q] = c_refs[q][...]

    def piece(q, carry):
        base = order_ref[q] * PIECE
        for a in range(2):
            cols = pl.ds(pl.multiple_of(base + a * 256, 256), 256)
            c = c_buf[q, :, a * 256 : (a + 1) * 256]
            accs = [loc_ref[h, :, cols] for h in range(HEADS)]
            for level in range(CROSS):
                r = jnp.dot(s_refs[level][...], c, preferred_element_type=F32)
                for h in range(HEADS):
                    here = slice(h * WIDTH, (h + 1) * WIDTH)
                    fac = fac_ref[level, h : h + 1, :]
                    row = sc_ref[1 + LOCAL + level, h : h + 1, cols] * jnp.concatenate([fac, fac], axis=1)
                    accs[h] = accs[h] + row * r[here, :]
            for h in range(HEADS):
                out_ref[h, :, cols] = accs[h].astype(BF16)
        return carry

    lax.fori_loop(0, PIECES, piece, 0)


def cross_part(order, loc, sc, fac, states, c_list):
    return pl.pallas_call(
        cross_kernel,
        out_shape=jax.ShapeDtypeStruct((HEADS, WIDTH, TOKENS), BF16),
        in_specs=[SMEM] + [VMEM] * (3 + CROSS + PIECES),
        out_specs=VMEM,
        scratch_shapes=[pltpu.VMEM((PIECES, STATE, PIECE), BF16)],
        compiler_params=params(),
        name="cross_part",
    )(order, loc, sc, fac, *states, *c_list)


def y_shift(x, k):
    return lax.ppermute(x, "head", [(i, ((i // 2 + k) % 4) * 2 + i % 2) for i in range(8)])


def other_core(x):
    return lax.ppermute(x, "head", [(i, i ^ 1) for i in range(8)])


def gather_pieces(x):
    near = [x] + [y_shift(x, k) for k in (1, 3, 2)]
    return near + [other_core(p) for p in near]


def partner(r, i):
    x, z = i // 8, i % 8
    if r == 0:
        z = z ^ 1
    elif r == 1:
        z = z ^ 2
    elif r == 2:
        z = 7 - z
    elif r == 3:
        x = x ^ 1
    else:
        x = 3 - x
    return x * 8 + z


def on_device(values, b_rows, c_rows, log_decay, level_weight):
    me = lax.axis_index("head")
    index = lax.axis_index("seq")
    y, core = me // 2, me % 2
    order = jnp.stack(
        [((y - k) % 4) * 2 + core for k in (0, 1, 3, 2)] + [((y - k) % 4) * 2 + 1 - core for k in (0, 1, 3, 2)]
    ).astype(jnp.int32)
    b_list = gather_pieces(b_rows)
    c_list = gather_pieces(c_rows)
    sc, binv, dec, grp = decay_rows(log_decay, level_weight)
    agg, own = block_states(order, values, dec, grp, b_list)
    loc = local_part(order, values, sc, binv, agg, b_list, c_list)
    states, facs = [], []
    before = jnp.zeros((HEADS, STATE), F32)
    for r in range(CROSS):
        got = lax.ppermute(own, "seq", [(i, partner(r, i)) for i in range(32)])
        right = ((index >> r) & 1) == 1
        states.append(got[:ROWS].astype(BF16))
        facs.append(jnp.where(right, jnp.exp(before), 0.0))
        if r == CROSS - 1:
            break
        own_tot = own[ROWS : ROWS + HEADS]
        got_tot = got[ROWS : ROWS + HEADS]
        scale = jnp.exp(jnp.where(right, own_tot, got_tot))
        scale = jnp.broadcast_to(scale[:, None], (HEADS, WIDTH, STATE)).reshape(ROWS, STATE)
        scale = jnp.concatenate([scale, jnp.ones((8, STATE), F32)], axis=0)
        own = scale * jnp.where(right, got, own) + jnp.where(right, own, got)
        before = before + jnp.where(right, got_tot, 0.0)
    fac = jnp.stack(facs)
    return cross_part(order, loc, sc, fac, states, c_list)


def solution(mesh):
    return jax.shard_map(
        on_device,
        mesh=mesh,
        in_specs=(
            P("head", None, "seq"),
            P(None, ("seq", "head")),
            P(None, ("seq", "head")),
            P("head", "seq"),
            P(None, "head", "seq"),
        ),
        out_specs=P("head", None, "seq"),
        check_vma=False,
    )
```

```python
import functools

import jax
import jax.numpy as jnp
from jax import lax
from jax.experimental import pallas as pl
from jax.experimental.pallas import tpu as pltpu
from jax.sharding import PartitionSpec as P

STRETCH = 64
HEADS = 3
WIDTH = 64
STATE = 128
ROWS = HEADS * WIDTH
PIECE = 512
PIECES = 8
TOKENS = PIECE * PIECES
LOCAL = 6
CROSS = 5
FIRST = (0, 32, 48, 56, 60, 62, 63)
HALF = PIECES // 2
U_STATE, U_LOCAL, U_CROSS = True, True, True
VMEM_LIMIT = 20 * 1024 * 1024
BINV, DEC, GRP = 12, 13, 14
F32 = jnp.float32
BF16 = jnp.bfloat16

VMEM = pl.BlockSpec(memory_space=pltpu.VMEM)
SMEM = pl.BlockSpec(memory_space=pltpu.SMEM)
ANY = pl.BlockSpec(memory_space=pl.ANY)


def params():
    return pltpu.CompilerParams(vmem_limit_bytes=VMEM_LIMIT)


def decay_kernel(ld_hbm, lw_hbm, *refs):
    out_ref, ld_ref, lw_ref, ld_sem, lw_sem = refs[-5:]
    ld_copy = pltpu.make_async_copy(ld_hbm, ld_ref, ld_sem)
    lw_copy = pltpu.make_async_copy(lw_hbm, lw_ref, lw_sem)
    ld_copy.start()
    lw_copy.start()
    ld_copy.wait()
    tiles = TOKENS // 128
    lane = lax.broadcasted_iota(jnp.int32, (HEADS, 128), 1)
    local = lane & 63

    def put_factor(slot, value):
        out_ref[GRP + slot // 32, :, pl.ds(slot % 32 * 128, 128)] = value

    runs, grows = [], []
    for i in range(tiles):
        cols = pl.ds(i * 128, 128)
        ld = ld_ref[:, cols]
        cum = ld
        for k in (1, 2, 4, 8, 16, 32):
            cum = cum + jnp.where(local >= k, pltpu.roll(cum, k, 1), 0.0)
        rest = ld
        for k in (1, 2, 4, 8, 16, 32):
            rest = rest + jnp.where(local < 64 - k, pltpu.roll(rest, 128 - k, 1), 0.0)
        grow = jnp.exp(cum)
        grows.append(grow)
        out_ref[DEC, :, cols] = jnp.exp(rest - ld)
        out_ref[BINV, :, cols] = jnp.exp(-cum)
        put_factor(i, jnp.broadcast_to(grow[:, 127:128], (HEADS, 128)))
        left = jnp.broadcast_to(cum[:, 63:64], (HEADS, 128))
        runs.append(cum + jnp.where(lane >= 64, left, 0.0))
    lw_copy.wait()
    for i in range(tiles):
        cols = pl.ds(i * 128, 128)
        out_ref[0, :, cols] = lw_ref[0, :, cols] * grows[i]
        out_ref[1, :, cols] = jnp.where(lane >= 64, lw_ref[1, :, cols] * grows[i], 0.0)
    for level in range(2, LOCAL + 2):
        span = 2 ** (level - 2)
        ends = [jnp.broadcast_to(runs[i][:, 127:128], (HEADS, 128)) for i in range(span - 1, tiles, span)]
        for i in range(tiles):
            cols = pl.ds(i * 128, 128)
            if level <= LOCAL:
                if (i // span) % 2:
                    out_ref[level, :, cols] = lw_ref[level, :, cols] * jnp.exp(runs[i])
                else:
                    out_ref[level, :, cols] = jnp.zeros((HEADS, 128), F32)
            else:
                grow = jnp.exp(runs[i])
                for up in range(CROSS):
                    out_ref[level + up, :, cols] = lw_ref[level + up, :, cols] * grow
        if level <= LOCAL:
            for i in range(tiles // (2 * span)):
                put_factor(FIRST[level - 1] + i, jnp.exp(ends[2 * i + 1]))
            for i in range(tiles):
                if (i // span) % 2:
                    runs[i] = runs[i] + ends[i // span - 1]
        else:
            put_factor(63, ends[0])


def decay_rows(log_decay, level_weight, after):
    return pl.pallas_call(
        decay_kernel,
        out_shape=jax.ShapeDtypeStruct((16, HEADS, TOKENS), F32),
        in_specs=[ANY] * (2 + len(after)),
        out_specs=VMEM,
        scratch_shapes=[
            pltpu.VMEM(log_decay.shape, F32),
            pltpu.VMEM(level_weight.shape, F32),
            pltpu.SemaphoreType.DMA,
            pltpu.SemaphoreType.DMA,
        ],
        compiler_params=params(),
        name="decay_rows",
    )(log_decay, level_weight, *after)


def stack_kernel(own_hbm, p1, p2, p3, *refs):
    out_ref, sem = refs[-2:]
    copy = pltpu.make_async_copy(own_hbm, out_ref.at[0], sem)
    copy.start()
    out_ref[1] = p1[...]
    out_ref[2] = p2[...]
    out_ref[3] = p3[...]
    copy.wait()


def stack(own, parts, after):
    return pl.pallas_call(
        stack_kernel,
        out_shape=jax.ShapeDtypeStruct((HALF, STATE, PIECE), BF16),
        in_specs=[ANY] + [VMEM] * 3 + [ANY] * len(after),
        out_specs=VMEM,
        scratch_shapes=[pltpu.SemaphoreType.DMA],
        compiler_params=params(),
        name="stack_pieces",
    )(own, *parts, *after)


def state_kernel(half, order_ref, v_ref, row_ref, b_ref, *refs):
    if half == 0:
        agg_ref, p_ref = refs
    else:
        p_old, agg_ref, tree_ref, end_ref, p_ref = refs
    lane = lax.broadcasted_iota(jnp.int32, (WIDTH, 128), 1)
    first = lane < 64

    def factor(h, slot):
        if isinstance(slot, int):
            return row_ref[GRP + slot // 32, h : h + 1, pl.ds(slot % 32 * 128, 128)]
        return row_ref[GRP + (slot >> 5), h : h + 1, pl.ds(pl.multiple_of((slot & 31) * 128, 128), 128)]

    def piece(q, carry):
        j = order_ref[half * HALF + q]
        for h in range(HEADS):
            here = slice(h * WIDTH, (h + 1) * WIDTH)
            tops = []
            for a in range(4):
                cols = pl.ds(pl.multiple_of(j * PIECE + a * 128, 128), 128)
                b = b_ref[q, :, a * 128 : (a + 1) * 128].astype(F32)
                v = v_ref[h, :, cols]
                keys = (row_ref[DEC, h : h + 1, cols] * b).astype(BF16)
                zero = jnp.zeros_like(v)
                both = jnp.concatenate([jnp.where(first, v, zero), jnp.where(first, zero, v)], axis=0)
                s = lax.dot_general(both, keys, (((1,), (1,)), ((), ())), preferred_element_type=F32)
                agg_ref[q, a, here, :] = s[:WIDTH].astype(BF16)
                tops.append(factor(h, j * 4 + a) * s[:WIDTH] + s[WIDTH:])
            agg_ref[q, 4, here, :] = tops[0].astype(BF16)
            agg_ref[q, 5, here, :] = tops[2].astype(BF16)
            lo = factor(h, FIRST[1] + j * 2) * tops[0] + tops[1]
            hi = factor(h, FIRST[1] + j * 2 + 1) * tops[2] + tops[3]
            agg_ref[q, 6, here, :] = lo.astype(BF16)
            p_ref[j, here, :] = factor(h, FIRST[2] + j) * lo + hi
        return carry

    lax.fori_loop(0, HALF, piece, 0, unroll=U_STATE)
    if half == 0:
        return
    for q in range(HALF):
        j = order_ref[q]
        p_ref[j] = p_old[j]
    for h in range(HEADS):
        here = slice(h * WIDTH, (h + 1) * WIDTH)
        tops = [p_ref[j, here, :] for j in range(PIECES)]
        for level in range(4, LOCAL + 1):
            nxt = []
            for i in range(len(tops) // 2):
                slot = FIRST[level - 1] + i
                tree_ref[slot - FIRST[3], here, :] = tops[2 * i].astype(BF16)
                nxt.append(factor(h, slot) * tops[2 * i] + tops[2 * i + 1])
            tops = nxt
        end_ref[here, :] = tops[0]
    end_ref[ROWS : ROWS + 8, :] = jnp.concatenate([row_ref[GRP + 1, :, 31 * 128 :], jnp.zeros((5, 128), F32)], axis=0)


def block_states(half, order, values, rows, b, old=()):
    agg = jax.ShapeDtypeStruct((HALF, 7, ROWS, STATE), BF16)
    tops = jax.ShapeDtypeStruct((PIECES, ROWS, STATE), F32)
    end = [jax.ShapeDtypeStruct((7, ROWS, STATE), BF16), jax.ShapeDtypeStruct((ROWS + 8, STATE), F32)]
    return pl.pallas_call(
        functools.partial(state_kernel, half),
        out_shape=[agg, tops] if half == 0 else [agg] + end,
        in_specs=[SMEM] + [VMEM] * (3 + len(old)),
        out_specs=[VMEM] * (2 if half == 0 else 3),
        scratch_shapes=[] if half == 0 else [pltpu.VMEM(tops.shape, F32)],
        compiler_params=params(),
        name="block_states",
    )(order, values, rows, b, *old)


def local_kernel(half, order_ref, v_ref, sc_ref, agg_ref, tree_ref, b_ref, c_ref, own_ref, *refs):
    out_ref, same_ref = refs[-2:]
    same_ref[...] = own_ref[...]
    s_id = lax.broadcasted_iota(jnp.int32, (128, 128), 0)
    t_id = lax.broadcasted_iota(jnp.int32, (128, 128), 1)
    keep = (s_id <= t_id) & ((s_id >> 6) == (t_id >> 6))

    def piece(q, carry):
        j = order_ref[half * HALF + q]
        base = j * PIECE
        for a in range(4):
            cols = pl.ds(pl.multiple_of(base + a * 128, 128), 128)
            mine = slice(a * 128, (a + 1) * 128)
            c = c_ref[q, :, mine]
            b = b_ref[q, :, mine]
            scores = lax.dot_general(b, c, (((0,), (0,)), ((), ())), preferred_element_type=F32)
            scores = jnp.where(keep, scores, 0.0)
            slots = [(1, a)]
            if a & 1:
                slots.append((2, 4 + a // 2))
            if a & 2:
                slots.append((3, 6))
            reads = [(level, jnp.dot(agg_ref[q, slot], c, preferred_element_type=F32)) for level, slot in slots]
            for h in range(HEADS):
                here = slice(h * WIDTH, (h + 1) * WIDTH)
                col = jnp.transpose(jnp.broadcast_to(sc_ref[BINV, h : h + 1, cols], (128, 128)))
                mix = ((sc_ref[0, h : h + 1, cols] * scores) * col).astype(BF16)
                acc = jnp.dot(v_ref[h, :, cols], mix, preferred_element_type=F32)
                for level, r in reads:
                    acc = acc + sc_ref[level, h : h + 1, cols] * r[here, :]
                out_ref[q, h, :, mine] = acc
        for level in range(4, LOCAL + 1):
            bit = level - 4

            @pl.when(((j >> bit) & 1) == 1)
            def _():
                slot = FIRST[level - 1] - FIRST[3] + (j >> (bit + 1))
                for a in range(2):
                    cols = pl.ds(pl.multiple_of(base + a * 256, 256), 256)
                    mine = slice(a * 256, (a + 1) * 256)
                    r = jnp.dot(tree_ref[slot], c_ref[q, :, mine], preferred_element_type=F32)
                    for h in range(HEADS):
                        here = slice(h * WIDTH, (h + 1) * WIDTH)
                        out_ref[q, h, :, mine] += sc_ref[level, h : h + 1, cols] * r[here, :]

        return carry

    lax.fori_loop(0, HALF, piece, 0, unroll=U_LOCAL)


def local_part(half, order, values, rows, agg, tree, b, c, own):
    return pl.pallas_call(
        functools.partial(local_kernel, half),
        out_shape=[
            jax.ShapeDtypeStruct((HALF, HEADS, WIDTH, PIECE), F32),
            jax.ShapeDtypeStruct(own.shape, own.dtype),
        ],
        in_specs=[SMEM] + [VMEM] * 7,
        out_specs=[VMEM] * 2,
        compiler_params=params(),
        name="local_part",
    )(order, values, rows, agg, tree, b, c, own)


def cross_kernel(rounds, last, order_ref, bits_ref, sc_ref, *refs):
    n = len(rounds)
    s_refs, pre_refs = refs[:n], refs[n : 2 * n]
    c_refs = refs[2 * n : 2 * n + 2]
    loc_refs = refs[2 * n + 2 : 2 * n + 4]
    outs = refs[2 * n + 4 :]
    if not last:
        own_ref, outs, same_ref = outs[0], outs[1:3], outs[3]
        same_ref[...] = own_ref[...]
    facs = []
    for k, r in enumerate(rounds):
        row = jnp.where(bits_ref[r] == 1, jnp.exp(pre_refs[k][:HEADS, :]), 0.0)
        facs.append(jnp.concatenate([row, row], axis=1))
    for g in range(2):

        def piece(q, carry):
            base = order_ref[g * HALF + q] * PIECE
            for a in range(2):
                cols = pl.ds(pl.multiple_of(base + a * 256, 256), 256)
                mine = slice(a * 256, (a + 1) * 256)
                c = c_refs[g][q, :, mine]
                accs = [loc_refs[g][q, h, :, mine] for h in range(HEADS)]
                for k, r in enumerate(rounds):
                    prod = jnp.dot(s_refs[k][...], c, preferred_element_type=F32)
                    for h in range(HEADS):
                        here = slice(h * WIDTH, (h + 1) * WIDTH)
                        row = sc_ref[1 + LOCAL + r, h : h + 1, cols] * facs[k][h : h + 1, :]
                        accs[h] = accs[h] + row * prod[here, :]
                for h in range(HEADS):
                    if last:
                        outs[0][h, :, cols] = accs[h].astype(BF16)
                    else:
                        outs[g][q, h, :, mine] = accs[h]
            return carry

        lax.fori_loop(0, HALF, piece, 0, unroll=U_CROSS)


def cross_part(rounds, order, bits, rows, states, pres, c_stacks, locs, own=None):
    last = own is None
    full = jax.ShapeDtypeStruct((HEADS, WIDTH, TOKENS), BF16)
    same = [jax.ShapeDtypeStruct(x.shape, x.dtype) for x in list(locs) + ([] if last else [own])]
    first_loc = 3 + 2 * len(rounds) + 2
    return pl.pallas_call(
        functools.partial(cross_kernel, rounds, last),
        out_shape=full if last else same,
        in_specs=[SMEM] * 2 + [VMEM] * (1 + 2 * len(rounds) + 4 + (0 if last else 1)),
        out_specs=VMEM if last else [VMEM] * 3,
        input_output_aliases={} if last else {first_loc + i: i for i in range(2)},
        compiler_params=params(),
        name="cross_part",
    )(order, bits, rows, *states, *pres, *c_stacks, *locs, *([] if last else [own]))


def combine(r, bits, own, got, pre):
    right = bits[r] == 1
    own_tot = own[ROWS:]
    got_tot = got[ROWS:]
    scale = jnp.exp(jnp.where(right, own_tot, got_tot))[:HEADS]
    scale = jnp.broadcast_to(scale[:, None], (HEADS, WIDTH, STATE)).reshape(ROWS, STATE)
    scale = jnp.concatenate([scale, jnp.ones((8, STATE), F32)], axis=0)
    new = scale * jnp.where(right, got, own) + jnp.where(right, own, got)
    if r == CROSS - 2:
        new = new[:ROWS].astype(BF16)
    return new, got[:ROWS].astype(BF16), pre + jnp.where(right, got_tot, 0.0)


def y_shift(x, k):
    return lax.ppermute(x, "head", [(i, ((i // 2 + k) % 4) * 2 + i % 2) for i in range(8)])


def other_core(x):
    return lax.ppermute(x, "head", [(i, i ^ 1) for i in range(8)])


def partner(r, i):
    x, z = i // 8, i % 8
    if r == 0:
        z = z ^ 1
    elif r == 1:
        z = z ^ 2
    elif r == 2:
        z = 7 - z
    elif r == 3:
        x = x ^ 1
    else:
        x = 3 - x
    return x * 8 + z


def exchange(r, x):
    return lax.ppermute(x, "seq", [(i, partner(r, i)) for i in range(32)])


def on_device(values, b_rows, c_rows, log_decay, level_weight):
    me = lax.axis_index("head")
    index = lax.axis_index("seq")
    q = lax.iota(jnp.int32, PIECES)
    turn = q & 3
    turn = turn ^ (turn >> 1)
    order = ((((me >> 1) - turn) & 3) << 1) | ((me & 1) ^ (q >> 2))
    bits = (index >> lax.iota(jnp.int32, CROSS)) & 1
    b1, c3 = y_shift(b_rows, 1), y_shift(c_rows, 3)
    b3, c1 = y_shift(b_rows, 3), y_shift(c_rows, 1)
    b2, c2 = y_shift(b1, 1), y_shift(c3, 3)
    rows = decay_rows(log_decay, level_weight, [b1, c3])
    b_near = stack(b_rows, [b1, b3, b2], [rows])
    b_far = other_core(b_near)
    c_near = stack(c_rows, [c1, c3, c2], [b_near])
    c_far = other_core(c_near)
    agg_near, tops = block_states(0, order, values, rows, b_near)
    agg_far, tree, own = block_states(1, order, values, rows, b_far, [tops])
    c_stacks = [c_near, c_far]
    pre = jnp.zeros((8, STATE), F32)
    pres, states, locs = [], [], []
    for r in range(CROSS):
        got = exchange(r, own)
        pres.append(pre)
        if r == 0:
            loc, own = local_part(0, order, values, rows, agg_near, tree, b_near, c_near, own)
            locs.append(loc)
        elif r == 1:
            loc, own = local_part(1, order, values, rows, agg_far, tree, b_far, c_far, own)
            locs.append(loc)
        elif r == 2:
            *locs, own = cross_part((0, 1), order, bits, rows, states, pres[:2], c_stacks, locs, own)
        elif r == 4:
            *locs, own = cross_part((2, 3), order, bits, rows, states[2:], pres[2:4], c_stacks, locs, own)
            return cross_part((4,), order, bits, rows, [got], [pre], c_stacks, locs)
        own, st, pre = combine(r, bits, own, got, pre)
        states.append(st)


def solution(mesh):
    return jax.shard_map(
        on_device,
        mesh=mesh,
        in_specs=(
            P("head", None, "seq"),
            P(None, ("seq", "head")),
            P(None, ("seq", "head")),
            P("head", "seq"),
            P(None, "head", "seq"),
        ),
        out_specs=P("head", None, "seq"),
        check_vma=False,
    )
```

```python
import functools

import jax
import jax.numpy as jnp
from jax import lax
from jax.experimental import pallas as pl
from jax.experimental.pallas import tpu as pltpu
from jax.sharding import PartitionSpec as P

STRETCH = 64
HEADS = 3
WIDTH = 64
STATE = 128
ROWS = HEADS * WIDTH
PIECE = 512
PIECES = 8
TOKENS = PIECE * PIECES
LOCAL = 6
CROSS = 5
FIRST = (0, 32, 48, 56, 60, 62, 63)
SHARES = ((), (0, 1, 2), (3, 4, 5, 6), (7,))
GROUPS = ((0, 1, 2), (3, 4, 5), (6,), (7,))
STEPS = ((0, 1, 2), (3, 4, 5), (6, 7))
VMEM_LIMIT = 20 * 1024 * 1024
BINV, DEC, GRP = 8, 9, 10
F32 = jnp.float32
BF16 = jnp.bfloat16

VMEM = pl.BlockSpec(memory_space=pltpu.VMEM)
SMEM = pl.BlockSpec(memory_space=pltpu.SMEM)
ANY = pl.BlockSpec(memory_space=pl.ANY)


def params():
    return pltpu.CompilerParams(vmem_limit_bytes=VMEM_LIMIT)


def cost(us):
    return pl.CostEstimate(flops=0, bytes_accessed=int(us * 3_500_000), transcendentals=0)


def decay_kernel(ld_ref, out_ref, run_ref):
    tiles = TOKENS // 128
    batch = 8
    lane = lax.broadcasted_iota(jnp.int32, (HEADS, 128), 1)
    local = lane & 63

    def first(g, carry):
        for i in range(batch):
            cols = pl.ds(pl.multiple_of(g * (batch * 128) + i * 128, 128), 128)
            ld = ld_ref[:, cols]
            cum = ld
            for k in (1, 2, 4, 8, 16, 32):
                cum = cum + jnp.where(local >= k, pltpu.roll(cum, k, 1), 0.0)
            rest = ld
            for k in (1, 2, 4, 8, 16, 32):
                rest = rest + jnp.where(local < 64 - k, pltpu.roll(rest, 128 - k, 1), 0.0)
            grow = jnp.exp(cum)
            out_ref[0, :, cols] = grow
            out_ref[1, :, cols] = jnp.where(lane >= 64, grow, 0.0)
            out_ref[DEC, :, cols] = jnp.exp(rest - ld)
            out_ref[BINV, :, cols] = jnp.exp(-cum)
            out_ref[GRP, :, cols] = jnp.broadcast_to(grow[:, 127:128], (HEADS, 128))
            left = jnp.broadcast_to(cum[:, 63:64], (HEADS, 128))
            run_ref[:, cols] = cum + jnp.where(lane >= 64, left, 0.0)
        return carry

    lax.fori_loop(0, tiles // batch, first, 0)
    runs = [run_ref[:, pl.ds(i * 128, 128)] for i in range(tiles)]
    for level in range(2, LOCAL + 2):
        span = 2 ** (level - 2)
        ends = [jnp.broadcast_to(runs[i][:, 127:128], (HEADS, 128)) for i in range(span - 1, tiles, span)]
        for i in range(tiles):
            cols = pl.ds(i * 128, 128)
            if level > LOCAL or (i // span) % 2:
                out_ref[level, :, cols] = jnp.exp(runs[i])
            else:
                out_ref[level, :, cols] = jnp.zeros((HEADS, 128), F32)
        if level <= LOCAL:
            for i in range(tiles // (2 * span)):
                slot = FIRST[level - 1] - 32 + i
                out_ref[GRP + 1, :, pl.ds(slot * 128, 128)] = jnp.exp(ends[2 * i + 1])
            for i in range(tiles):
                if (i // span) % 2:
                    runs[i] = runs[i] + ends[i // span - 1]
        else:
            out_ref[GRP + 1, :, pl.ds(31 * 128, 128)] = ends[0]


def decay_rows(log_decay):
    return pl.pallas_call(
        decay_kernel,
        out_shape=jax.ShapeDtypeStruct((12, HEADS, TOKENS), F32),
        in_specs=[VMEM],
        out_specs=VMEM,
        scratch_shapes=[pltpu.VMEM(log_decay.shape, F32)],
        compiler_params=params(),
        cost_estimate=cost(2),
        name="decay_rows",
    )(log_decay)


def hold_kernel(n, *refs):
    for x_ref, out_ref in zip(refs[:n], refs[-n:]):
        out_ref[...] = x_ref[...]


def hold(xs, after):
    n = len(xs)
    return pl.pallas_call(
        functools.partial(hold_kernel, n),
        out_shape=[jax.ShapeDtypeStruct(x.shape, x.dtype) for x in xs],
        in_specs=[VMEM] * n + [ANY] * len(after),
        out_specs=[VMEM] * n,
        compiler_params=params(),
        cost_estimate=cost(0.2),
        name="hold",
    )(*xs, *after)


def stack_kernel(p0, p1, p2, *refs):
    out_ref = refs[-1]
    out_ref[0] = p0[...]
    out_ref[1] = p1[...]
    out_ref[2] = p2[...]


def stack(parts, after):
    return pl.pallas_call(
        stack_kernel,
        out_shape=jax.ShapeDtypeStruct((3, STATE, PIECE), BF16),
        in_specs=[VMEM] * 3 + [ANY] * len(after),
        out_specs=VMEM,
        compiler_params=params(),
        cost_estimate=cost(0.2),
        name="stack_pieces",
    )(*parts, *after)


def state_kernel(group, order_ref, v_ref, row_ref, *refs):
    pieces = STEPS[group]
    last = group == len(STEPS) - 1
    b_refs = refs[: len(pieces)]
    if last:
        old_refs = refs[len(pieces) : len(pieces) + group]
        agg_ref, tree_ref, end_ref, p_ref = refs[-4:]
    else:
        agg_ref, top_ref = refs[-2:]
    lane = lax.broadcasted_iota(jnp.int32, (WIDTH, 128), 1)
    first = lane < 64

    def factor(h, slot):
        if isinstance(slot, int):
            return row_ref[GRP + slot // 32, h : h + 1, pl.ds(slot % 32 * 128, 128)]
        return row_ref[GRP + (slot >> 5), h : h + 1, pl.ds(pl.multiple_of((slot & 31) * 128, 128), 128)]

    for q, k in enumerate(pieces):
        j = order_ref[k]
        for h in range(HEADS):
            here = slice(h * WIDTH, (h + 1) * WIDTH)
            tops = []
            for a in range(4):
                cols = pl.ds(pl.multiple_of(j * PIECE + a * 128, 128), 128)
                b = b_refs[q][:, a * 128 : (a + 1) * 128].astype(F32)
                v = v_ref[h, :, cols]
                keys = (row_ref[DEC, h : h + 1, cols] * b).astype(BF16)
                zero = jnp.zeros_like(v)
                both = jnp.concatenate([jnp.where(first, v, zero), jnp.where(first, zero, v)], axis=0)
                s = lax.dot_general(both, keys, (((1,), (1,)), ((), ())), preferred_element_type=F32)
                agg_ref[q, a, here, :] = s[:WIDTH].astype(BF16)
                tops.append(factor(h, j * 4 + a) * s[:WIDTH] + s[WIDTH:])
            agg_ref[q, 4, here, :] = tops[0].astype(BF16)
            agg_ref[q, 5, here, :] = tops[2].astype(BF16)
            lo = factor(h, FIRST[1] + j * 2) * tops[0] + tops[1]
            hi = factor(h, FIRST[1] + j * 2 + 1) * tops[2] + tops[3]
            agg_ref[q, 6, here, :] = lo.astype(BF16)
            top = factor(h, FIRST[2] + j) * lo + hi
            if last:
                p_ref[j, here, :] = top
            else:
                top_ref[q, here, :] = top
    if not last:
        return
    for g, old in enumerate(old_refs):
        for q, k in enumerate(STEPS[g]):
            p_ref[order_ref[k]] = old[q]
    for h in range(HEADS):
        here = slice(h * WIDTH, (h + 1) * WIDTH)
        tops = [p_ref[j, here, :] for j in range(PIECES)]
        for level in range(4, LOCAL + 1):
            nxt = []
            for i in range(len(tops) // 2):
                slot = FIRST[level - 1] + i
                tree_ref[slot - FIRST[3], here, :] = tops[2 * i].astype(BF16)
                nxt.append(factor(h, slot) * tops[2 * i] + tops[2 * i + 1])
            tops = nxt
        end_ref[here, :] = tops[0]
    end_ref[ROWS : ROWS + 8, :] = jnp.concatenate([row_ref[GRP + 1, :, 31 * 128 :], jnp.zeros((5, 128), F32)], axis=0)


def block_states(group, order, values, rows, b_list, old=(), after=()):
    n = len(STEPS[group])
    agg = jax.ShapeDtypeStruct((n, 7, ROWS, STATE), BF16)
    tops = jax.ShapeDtypeStruct((n, ROWS, STATE), F32)
    end = [jax.ShapeDtypeStruct((7, ROWS, STATE), BF16), jax.ShapeDtypeStruct((ROWS + 8, STATE), F32)]
    last = group == len(STEPS) - 1
    return pl.pallas_call(
        functools.partial(state_kernel, group),
        out_shape=[agg] + (end if last else [tops]),
        in_specs=[SMEM] + [VMEM] * (2 + len(b_list) + len(old)) + [ANY] * len(after),
        out_specs=[VMEM] * (3 if last else 2),
        scratch_shapes=[pltpu.VMEM((PIECES, ROWS, STATE), F32)] if last else [],
        compiler_params=params(),
        cost_estimate=cost(1.5),
        name="block_states",
    )(order, values, rows, *b_list, *old, *after)


def home(piece):
    for g, group in enumerate(GROUPS):
        if piece in group:
            return g, group.index(piece)


def local_kernel(pieces, order_ref, v_ref, row_ref, lw_ref, tree_ref, own_ref, *refs):
    out_ref, same_ref = refs[-2:]
    same_ref[...] = own_ref[...]
    used = sorted({home(k)[0] for k in pieces})
    s_id = lax.broadcasted_iota(jnp.int32, (128, 128), 0)
    t_id = lax.broadcasted_iota(jnp.int32, (128, 128), 1)
    keep = (s_id <= t_id) & ((s_id >> 6) == (t_id >> 6))
    for at, k in enumerate(pieces):
        g, q = home(k)
        b_ref = refs[at]
        agg_ref, c_ref = refs[len(pieces) + 2 * used.index(g) :][:2]
        j = order_ref[k]
        for a in range(4):
            cols = pl.ds(pl.multiple_of(j * PIECE + a * 128, 128), 128)
            mine = slice(a * 128, (a + 1) * 128)
            c = c_ref[q, :, mine]
            b = b_ref[:, mine]
            scores = lax.dot_general(b, c, (((0,), (0,)), ((), ())), preferred_element_type=F32)
            scores = jnp.where(keep, scores, 0.0)
            n = 1 if g == 3 else q
            slots = [(1, agg_ref[n, a])]
            if a & 1:
                slots.append((2, agg_ref[n, 4 + a // 2]))
            if a & 2:
                slots.append((3, agg_ref[n, 6]))
            for level in range(4, LOCAL + 1):
                slots.append((level, tree_ref[FIRST[level - 1] - FIRST[3] + (j >> (level - 3))]))
            every = jnp.dot(jnp.concatenate([x for _, x in slots], axis=0), c, preferred_element_type=F32)
            for h in range(HEADS):
                col = jnp.transpose(jnp.broadcast_to(row_ref[BINV, h : h + 1, cols], (128, 128)))
                mix = ((lw_ref[0, h : h + 1, cols] * row_ref[0, h : h + 1, cols] * scores) * col).astype(BF16)
                acc = jnp.dot(v_ref[h, :, cols], mix, preferred_element_type=F32)
                for i, (level, _) in enumerate(slots):
                    read = every[i * ROWS + h * WIDTH : i * ROWS + (h + 1) * WIDTH]
                    acc = acc + lw_ref[level, h : h + 1, cols] * row_ref[level, h : h + 1, cols] * read
                out_ref[at, h, :, mine] = acc


def local_part(pieces, order, values, rows, weights, tree, own, aggs, b_list, c_stacks):
    used = sorted({home(k)[0] for k in pieces})
    parts = [b_list[k] for k in pieces] + [x[i] for i in used for x in (aggs, c_stacks)]
    return pl.pallas_call(
        functools.partial(local_kernel, pieces),
        out_shape=[
            jax.ShapeDtypeStruct((len(pieces), HEADS, WIDTH, PIECE), F32),
            jax.ShapeDtypeStruct(own.shape, own.dtype),
        ],
        in_specs=[SMEM] + [VMEM] * (5 + len(parts)),
        out_specs=[VMEM] * 2,
        compiler_params=params(),
        cost_estimate=cost(len(pieces)),
        name="local_part",
    )(order, values, rows, weights, tree, own, *parts)


def cross_kernel(rounds, sizes, last, order_ref, bits_ref, row_ref, lw_ref, *refs):
    n, m = len(rounds), len(sizes)
    s_refs, pre_refs = refs[:n], refs[n : 2 * n]
    w = len(GROUPS)
    c_refs = refs[2 * n : 2 * n + w]
    loc_refs = refs[2 * n + w : 2 * n + w + m]
    outs = refs[2 * n + w + m :]
    if last:
        full_ref, stage, sems = outs
    else:
        own_ref, outs, same_ref = outs[0], outs[1 : 1 + m], outs[1 + m :]
        if same_ref:
            same_ref[0][...] = own_ref[...]

    def send(k):
        cols = pl.ds(pl.multiple_of(order_ref[k] * PIECE, PIECE), PIECE)
        return pltpu.make_async_copy(stage.at[k], full_ref.at[:, :, cols], sems.at[k])

    facs = []
    for k, r in enumerate(rounds):
        row = jnp.where(bits_ref[r] == 1, jnp.exp(pre_refs[k][:HEADS, :]), 0.0)
        facs.append(jnp.concatenate([row, row], axis=1))
    states = jnp.concatenate([x[...] for x in s_refs], axis=0)
    place = [(g, o) for g in range(m) for o in range(sizes[g])]
    for q, (g, o) in enumerate(place):
        cg, ci = home(q)
        for a in range(2):
            cols = pl.ds(pl.multiple_of(order_ref[q] * PIECE + a * 256, 256), 256)
            mine = slice(a * 256, (a + 1) * 256)
            every = jnp.dot(states, c_refs[cg][ci, :, mine], preferred_element_type=F32)
            for h in range(HEADS):
                acc = loc_refs[g][o, h, :, mine]
                grow = row_ref[1 + LOCAL, h : h + 1, cols]
                for k, r in enumerate(rounds):
                    row = lw_ref[1 + LOCAL + r, h : h + 1, cols] * grow * facs[k][h : h + 1, :]
                    acc = acc + row * every[k * ROWS + h * WIDTH : k * ROWS + (h + 1) * WIDTH]
                if last:
                    stage[q, h, :, mine] = acc.astype(BF16)
                else:
                    outs[g][o, h, :, mine] = acc
        if last:
            send(q).start()
    if last:
        for q in range(PIECES):
            send(q).wait()


def cross_part(rounds, order, bits, rows, weights, states, pres, c_stacks, locs, own=None, back=True):
    last = own is None
    full = jax.ShapeDtypeStruct((HEADS, WIDTH, TOKENS), BF16)
    same = [jax.ShapeDtypeStruct(x.shape, x.dtype) for x in list(locs) + ([own] if back and not last else [])]
    first_loc = 4 + 2 * len(rounds) + len(GROUPS)
    m = len(locs)
    owns = [] if last else [VMEM if back else ANY]
    return pl.pallas_call(
        functools.partial(cross_kernel, rounds, tuple(x.shape[0] for x in locs), last),
        out_shape=full if last else same,
        in_specs=[SMEM] * 2 + [VMEM] * (2 + 2 * len(rounds) + len(GROUPS) + m) + owns,
        out_specs=ANY if last else [VMEM] * len(same),
        scratch_shapes=[
            pltpu.VMEM((PIECES, HEADS, WIDTH, PIECE), BF16),
            pltpu.SemaphoreType.DMA((PIECES,)),
        ]
        if last
        else [],
        input_output_aliases={} if last else {first_loc + i: i for i in range(m)},
        compiler_params=params(),
        cost_estimate=cost(1 + len(rounds)),
        name="cross_part",
    )(order, bits, rows, weights, *states, *pres, *c_stacks, *locs, *([] if last else [own]))


def combine(r, bits, own, got, pre):
    right = bits[r] == 1
    own_tot = own[ROWS:]
    got_tot = got[ROWS:]
    scale = jnp.exp(jnp.where(right, own_tot, got_tot))[:HEADS]
    scale = jnp.broadcast_to(scale[:, None], (HEADS, WIDTH, STATE)).reshape(ROWS, STATE)
    scale = jnp.concatenate([scale, jnp.ones((8, STATE), F32)], axis=0)
    new = scale * jnp.where(right, got, own) + jnp.where(right, own, got)
    return new, got[:ROWS].astype(BF16), pre + jnp.where(right, got_tot, 0.0)


def y_shift(x, k):
    return lax.ppermute(x, "head", [(i, ((i // 2 + k) % 4) * 2 + i % 2) for i in range(8)])


def other_core(x):
    return lax.ppermute(x, "head", [(i, i ^ 1) for i in range(8)])


def partner(r, i):
    x, z = i // 8, i % 8
    if r == 0:
        z = z ^ 1
    elif r == 1:
        z = z ^ 2
    elif r == 2:
        z = 7 - z
    elif r == 3:
        x = x ^ 1
    else:
        x = 3 - x
    return x * 8 + z


def exchange(r, x):
    return lax.ppermute(x, "seq", [(i, partner(r, i)) for i in range(32)])


def on_device(values, b_rows, c_rows, log_decay, level_weight):
    me = lax.axis_index("head")
    index = lax.axis_index("seq")
    q = lax.iota(jnp.int32, PIECES)
    far = jnp.where(q < 6, (q >= 3).astype(jnp.int32), q & 1)
    near = q - 3 * far
    turn = jnp.where(q < 6, near + (near >> 1), 2)
    order = ((((me >> 1) - turn) & 3) << 1) | ((me & 1) ^ far)
    bits = (index >> lax.iota(jnp.int32, CROSS)) & 1
    b1, b3, b2 = (y_shift(b_rows, k) for k in (1, 3, 2))
    rows = decay_rows(log_decay)
    near = [*hold([b_rows, b1, b3], [rows]), b2]
    near_far = [other_core(x) for x in near]
    b_list = near[:3] + near_far[:3] + [near[3], near_far[3]]
    agg_a, top_a = block_states(0, order, values, rows, b_list[:3])
    agg_b, top_b = block_states(1, order, values, rows, b_list[3:6], (), [top_a])
    agg_c, tree, own = block_states(2, order, values, rows, b_list[6:], [top_a, top_b])
    (c_own,) = hold([c_rows], [rows])
    c1, c3 = y_shift(c_own, 1), y_shift(c_own, 3)
    c2 = y_shift(c3, 3)
    c_a = stack([c_own, c1, c3], [])
    c_b = other_core(c_a)
    c_d = other_core(c2)
    c_stacks = [c_a, c_b, c2[None], c_d[None]]
    stacks = ([agg_a, agg_b, agg_c, agg_c], b_list, c_stacks)
    local_args = (order, values, rows, level_weight, tree)
    cross_args = (order, bits, rows, level_weight)
    pre = jnp.zeros((8, STATE), F32)
    pres, states, locs = [], [], []
    for r in range(CROSS):
        sent = own if r < CROSS - 1 else own[:ROWS].astype(BF16)
        got = exchange(r, sent)
        pres.append(pre)
        if r < CROSS - 1 and SHARES[r]:
            loc, own = local_part(SHARES[r], *local_args, own, *stacks)
            locs.append(loc)
        elif r == CROSS - 1:
            locs = cross_part((0, 1, 2, 3), *cross_args, states, pres[:4], c_stacks, locs, sent, False)
            return cross_part((4,), *cross_args, [got], [pre], c_stacks, locs)
        own, st, pre = combine(r, bits, own, got, pre)
        states.append(st)


def solution(mesh):
    return jax.shard_map(
        on_device,
        mesh=mesh,
        in_specs=(
            P("head", None, "seq"),
            P(None, ("seq", "head")),
            P(None, ("seq", "head")),
            P("head", "seq"),
            P(None, "head", "seq"),
        ),
        out_specs=P("head", None, "seq"),
        check_vma=False,
    )
```

```python
import functools

import jax
import jax.numpy as jnp
from jax import lax
from jax.experimental import pallas as pl
from jax.experimental.pallas import tpu as pltpu
from jax.sharding import PartitionSpec as P

STRETCH = 64
HEADS = 3
WIDTH = 64
STATE = 128
ROWS = HEADS * WIDTH
PIECE = 512
PIECES = 8
TOKENS = PIECE * PIECES
LOCAL = 6
CROSS = 5
FIRST = (0, 32, 48, 56, 60, 62, 63)
SHARES = ((), (0, 1, 2), (3, 4, 5), (6, 7))
GROUPS = ((0, 1, 2), (3, 4, 5), (6,), (7,))
STEPS = ((0, 1, 2), (3, 4, 5, 6, 7))
VMEM_LIMIT = 20 * 1024 * 1024
BINV, DEC, GRP = 8, 9, 10
F32 = jnp.float32
BF16 = jnp.bfloat16

VMEM = pl.BlockSpec(memory_space=pltpu.VMEM)
SMEM = pl.BlockSpec(memory_space=pltpu.SMEM)
ANY = pl.BlockSpec(memory_space=pl.ANY)


def params():
    return pltpu.CompilerParams(vmem_limit_bytes=VMEM_LIMIT)


def cost(us):
    return pl.CostEstimate(flops=0, bytes_accessed=int(us * 3_500_000), transcendentals=0)


def decay_kernel(ld_ref, out_ref, run_ref):
    tiles = TOKENS // 128
    batch = 8
    lane = lax.broadcasted_iota(jnp.int32, (HEADS, 128), 1)
    local = lane & 63

    def first(g, carry):
        for i in range(batch):
            cols = pl.ds(pl.multiple_of(g * (batch * 128) + i * 128, 128), 128)
            ld = ld_ref[:, cols]
            cum = ld
            for k in (1, 2, 4, 8, 16, 32):
                cum = cum + jnp.where(local >= k, pltpu.roll(cum, k, 1), 0.0)
            rest = ld
            for k in (1, 2, 4, 8, 16, 32):
                rest = rest + jnp.where(local < 64 - k, pltpu.roll(rest, 128 - k, 1), 0.0)
            grow = jnp.exp(cum)
            out_ref[0, :, cols] = grow
            out_ref[1, :, cols] = jnp.where(lane >= 64, grow, 0.0)
            out_ref[DEC, :, cols] = jnp.exp(rest - ld)
            out_ref[BINV, :, cols] = jnp.exp(-cum)
            out_ref[GRP, :, cols] = jnp.broadcast_to(grow[:, 127:128], (HEADS, 128))
            left = jnp.broadcast_to(cum[:, 63:64], (HEADS, 128))
            run_ref[:, cols] = cum + jnp.where(lane >= 64, left, 0.0)
        return carry

    lax.fori_loop(0, tiles // batch, first, 0)
    runs = [run_ref[:, pl.ds(i * 128, 128)] for i in range(tiles)]
    for level in range(2, LOCAL + 2):
        span = 2 ** (level - 2)
        ends = [jnp.broadcast_to(runs[i][:, 127:128], (HEADS, 128)) for i in range(span - 1, tiles, span)]
        for i in range(tiles):
            cols = pl.ds(i * 128, 128)
            if level > LOCAL or (i // span) % 2:
                out_ref[level, :, cols] = jnp.exp(runs[i])
            else:
                out_ref[level, :, cols] = jnp.zeros((HEADS, 128), F32)
        if level <= LOCAL:
            for i in range(tiles // (2 * span)):
                slot = FIRST[level - 1] - 32 + i
                out_ref[GRP + 1, :, pl.ds(slot * 128, 128)] = jnp.exp(ends[2 * i + 1])
            for i in range(tiles):
                if (i // span) % 2:
                    runs[i] = runs[i] + ends[i // span - 1]
        else:
            out_ref[GRP + 1, :, pl.ds(31 * 128, 128)] = ends[0]


def decay_rows(log_decay):
    return pl.pallas_call(
        decay_kernel,
        out_shape=jax.ShapeDtypeStruct((12, HEADS, TOKENS), F32),
        in_specs=[VMEM],
        out_specs=VMEM,
        scratch_shapes=[pltpu.VMEM(log_decay.shape, F32)],
        compiler_params=params(),
        cost_estimate=cost(2),
        name="decay_rows",
    )(log_decay)


def hold_kernel(n, *refs):
    for x_ref, out_ref in zip(refs[:n], refs[-n:]):
        out_ref[...] = x_ref[...]


def hold(xs, after):
    n = len(xs)
    return pl.pallas_call(
        functools.partial(hold_kernel, n),
        out_shape=[jax.ShapeDtypeStruct(x.shape, x.dtype) for x in xs],
        in_specs=[VMEM] * n + [ANY] * len(after),
        out_specs=[VMEM] * n,
        compiler_params=params(),
        cost_estimate=cost(0.2),
        name="hold",
    )(*xs, *after)


def stack_kernel(p0, p1, p2, *refs):
    out_ref = refs[-1]
    out_ref[0] = p0[...]
    out_ref[1] = p1[...]
    out_ref[2] = p2[...]


def stack(parts, after):
    return pl.pallas_call(
        stack_kernel,
        out_shape=jax.ShapeDtypeStruct((3, STATE, PIECE), BF16),
        in_specs=[VMEM] * 3 + [ANY] * len(after),
        out_specs=VMEM,
        compiler_params=params(),
        cost_estimate=cost(0.2),
        name="stack_pieces",
    )(*parts, *after)


def state_kernel(group, order_ref, v_ref, row_ref, *refs):
    pieces = STEPS[group]
    last = group == len(STEPS) - 1
    b_refs = refs[: len(pieces)]
    if last:
        old_refs = refs[len(pieces) : len(pieces) + group]
        agg_ref, tree_ref, end_ref, p_ref = refs[-4:]
    else:
        agg_ref, top_ref = refs[-2:]
    lane = lax.broadcasted_iota(jnp.int32, (WIDTH, 128), 1)
    first = lane < 64

    def factor(h, slot):
        if isinstance(slot, int):
            return row_ref[GRP + slot // 32, h : h + 1, pl.ds(slot % 32 * 128, 128)]
        return row_ref[GRP + (slot >> 5), h : h + 1, pl.ds(pl.multiple_of((slot & 31) * 128, 128), 128)]

    for q, k in enumerate(pieces):
        j = order_ref[k]
        for h in range(HEADS):
            here = slice(h * WIDTH, (h + 1) * WIDTH)
            tops = []
            for a in range(4):
                cols = pl.ds(pl.multiple_of(j * PIECE + a * 128, 128), 128)
                b = b_refs[q][:, a * 128 : (a + 1) * 128].astype(F32)
                v = v_ref[h, :, cols]
                keys = (row_ref[DEC, h : h + 1, cols] * b).astype(BF16)
                zero = jnp.zeros_like(v)
                both = jnp.concatenate([jnp.where(first, v, zero), jnp.where(first, zero, v)], axis=0)
                s = lax.dot_general(both, keys, (((1,), (1,)), ((), ())), preferred_element_type=F32)
                agg_ref[q, a, here, :] = s[:WIDTH].astype(BF16)
                tops.append(factor(h, j * 4 + a) * s[:WIDTH] + s[WIDTH:])
            agg_ref[q, 4, here, :] = tops[0].astype(BF16)
            agg_ref[q, 5, here, :] = tops[2].astype(BF16)
            lo = factor(h, FIRST[1] + j * 2) * tops[0] + tops[1]
            hi = factor(h, FIRST[1] + j * 2 + 1) * tops[2] + tops[3]
            agg_ref[q, 6, here, :] = lo.astype(BF16)
            top = factor(h, FIRST[2] + j) * lo + hi
            if last:
                p_ref[j, here, :] = top
            else:
                top_ref[q, here, :] = top
    if not last:
        return
    for g, old in enumerate(old_refs):
        for q, k in enumerate(STEPS[g]):
            p_ref[order_ref[k]] = old[q]
    for h in range(HEADS):
        here = slice(h * WIDTH, (h + 1) * WIDTH)
        tops = [p_ref[j, here, :] for j in range(PIECES)]
        for level in range(4, LOCAL + 1):
            nxt = []
            for i in range(len(tops) // 2):
                slot = FIRST[level - 1] + i
                tree_ref[slot - FIRST[3], here, :] = tops[2 * i].astype(BF16)
                nxt.append(factor(h, slot) * tops[2 * i] + tops[2 * i + 1])
            tops = nxt
        end_ref[here, :] = tops[0]
    end_ref[ROWS : ROWS + 8, :] = jnp.concatenate([row_ref[GRP + 1, :, 31 * 128 :], jnp.zeros((5, 128), F32)], axis=0)


def block_states(group, order, values, rows, b_list, old=(), after=()):
    n = len(STEPS[group])
    agg = jax.ShapeDtypeStruct((n, 7, ROWS, STATE), BF16)
    tops = jax.ShapeDtypeStruct((n, ROWS, STATE), F32)
    end = [jax.ShapeDtypeStruct((7, ROWS, STATE), BF16), jax.ShapeDtypeStruct((ROWS + 8, STATE), F32)]
    last = group == len(STEPS) - 1
    return pl.pallas_call(
        functools.partial(state_kernel, group),
        out_shape=[agg] + (end if last else [tops]),
        in_specs=[SMEM] + [VMEM] * (2 + len(b_list) + len(old)) + [ANY] * len(after),
        out_specs=[VMEM] * (3 if last else 2),
        scratch_shapes=[pltpu.VMEM((PIECES, ROWS, STATE), F32)] if last else [],
        compiler_params=params(),
        cost_estimate=cost(1.5),
        name="block_states",
    )(order, values, rows, *b_list, *old, *after)


def home(piece):
    for g, group in enumerate(GROUPS):
        if piece in group:
            return g, group.index(piece)


def local_kernel(pieces, order_ref, v_ref, row_ref, lw_ref, tree_ref, own_ref, *refs):
    out_ref, same_ref = refs[-2:]
    same_ref[...] = own_ref[...]
    used = sorted({home(k)[0] for k in pieces})
    s_id = lax.broadcasted_iota(jnp.int32, (128, 128), 0)
    t_id = lax.broadcasted_iota(jnp.int32, (128, 128), 1)
    keep = (s_id <= t_id) & ((s_id >> 6) == (t_id >> 6))
    for at, k in enumerate(pieces):
        g, q = home(k)
        b_ref = refs[at]
        agg_ref, c_ref = refs[len(pieces) + 2 * used.index(g) :][:2]
        j = order_ref[k]
        for a in range(4):
            cols = pl.ds(pl.multiple_of(j * PIECE + a * 128, 128), 128)
            mine = slice(a * 128, (a + 1) * 128)
            c = c_ref[q, :, mine]
            b = b_ref[:, mine]
            scores = lax.dot_general(b, c, (((0,), (0,)), ((), ())), preferred_element_type=F32)
            scores = jnp.where(keep, scores, 0.0)
            n = k - GROUPS[min(g, 1)][0]
            slots = [(1, agg_ref[n, a])]
            if a & 1:
                slots.append((2, agg_ref[n, 4 + a // 2]))
            if a & 2:
                slots.append((3, agg_ref[n, 6]))
            for level in range(4, LOCAL + 1):
                slots.append((level, tree_ref[FIRST[level - 1] - FIRST[3] + (j >> (level - 3))]))
            every = jnp.dot(jnp.concatenate([x for _, x in slots], axis=0), c, preferred_element_type=F32)
            for h in range(HEADS):
                col = jnp.transpose(jnp.broadcast_to(row_ref[BINV, h : h + 1, cols], (128, 128)))
                mix = ((lw_ref[0, h : h + 1, cols] * row_ref[0, h : h + 1, cols] * scores) * col).astype(BF16)
                acc = jnp.dot(v_ref[h, :, cols], mix, preferred_element_type=F32)
                for i, (level, _) in enumerate(slots):
                    read = every[i * ROWS + h * WIDTH : i * ROWS + (h + 1) * WIDTH]
                    acc = acc + lw_ref[level, h : h + 1, cols] * row_ref[level, h : h + 1, cols] * read
                out_ref[at, h, :, mine] = acc


def local_part(pieces, order, values, rows, weights, tree, own, aggs, b_list, c_stacks):
    used = sorted({home(k)[0] for k in pieces})
    parts = [b_list[k] for k in pieces] + [x[i] for i in used for x in (aggs, c_stacks)]
    return pl.pallas_call(
        functools.partial(local_kernel, pieces),
        out_shape=[
            jax.ShapeDtypeStruct((len(pieces), HEADS, WIDTH, PIECE), F32),
            jax.ShapeDtypeStruct(own.shape, own.dtype),
        ],
        in_specs=[SMEM] + [VMEM] * (5 + len(parts)),
        out_specs=[VMEM] * 2,
        compiler_params=params(),
        cost_estimate=cost(len(pieces)),
        name="local_part",
    )(order, values, rows, weights, tree, own, *parts)


def cross_kernel(rounds, sizes, last, order_ref, bits_ref, row_ref, lw_ref, *refs):
    n, m = len(rounds), len(sizes)
    s_refs, pre_refs = refs[:n], refs[n : 2 * n]
    w = len(GROUPS)
    c_refs = refs[2 * n : 2 * n + w]
    loc_refs = refs[2 * n + w : 2 * n + w + m]
    outs = refs[2 * n + w + m :]
    if last:
        full_ref, stage, sems = outs
    else:
        own_ref, outs, same_ref = outs[0], outs[1 : 1 + m], outs[1 + m :]
        if same_ref:
            same_ref[0][...] = own_ref[...]

    def send(k):
        cols = pl.ds(pl.multiple_of(order_ref[k] * PIECE, PIECE), PIECE)
        return pltpu.make_async_copy(stage.at[k], full_ref.at[:, :, cols], sems.at[k])

    facs = []
    for k, r in enumerate(rounds):
        row = jnp.where(bits_ref[r] == 1, jnp.exp(pre_refs[k][:HEADS, :]), 0.0)
        facs.append(jnp.concatenate([row, row], axis=1))
    states = jnp.concatenate([x[...] for x in s_refs], axis=0)
    place = [(g, o) for g in range(m) for o in range(sizes[g])]
    for q, (g, o) in enumerate(place):
        cg, ci = home(q)
        for a in range(2):
            cols = pl.ds(pl.multiple_of(order_ref[q] * PIECE + a * 256, 256), 256)
            mine = slice(a * 256, (a + 1) * 256)
            every = jnp.dot(states, c_refs[cg][ci, :, mine], preferred_element_type=F32)
            for h in range(HEADS):
                acc = loc_refs[g][o, h, :, mine]
                grow = row_ref[1 + LOCAL, h : h + 1, cols]
                for k, r in enumerate(rounds):
                    row = lw_ref[1 + LOCAL + r, h : h + 1, cols] * grow * facs[k][h : h + 1, :]
                    acc = acc + row * every[k * ROWS + h * WIDTH : k * ROWS + (h + 1) * WIDTH]
                if last:
                    stage[q, h, :, mine] = acc.astype(BF16)
                else:
                    outs[g][o, h, :, mine] = acc
        if last:
            send(q).start()
    if last:
        for q in range(PIECES):
            send(q).wait()


def cross_part(rounds, order, bits, rows, weights, states, pres, c_stacks, locs, own=None, back=True):
    last = own is None
    full = jax.ShapeDtypeStruct((HEADS, WIDTH, TOKENS), BF16)
    same = [jax.ShapeDtypeStruct(x.shape, x.dtype) for x in list(locs) + ([own] if back and not last else [])]
    first_loc = 4 + 2 * len(rounds) + len(GROUPS)
    m = len(locs)
    owns = [] if last else [VMEM if back else ANY]
    return pl.pallas_call(
        functools.partial(cross_kernel, rounds, tuple(x.shape[0] for x in locs), last),
        out_shape=full if last else same,
        in_specs=[SMEM] * 2 + [VMEM] * (2 + 2 * len(rounds) + len(GROUPS) + m) + owns,
        out_specs=ANY if last else [VMEM] * len(same),
        scratch_shapes=[
            pltpu.VMEM((PIECES, HEADS, WIDTH, PIECE), BF16),
            pltpu.SemaphoreType.DMA((PIECES,)),
        ]
        if last
        else [],
        input_output_aliases={} if last else {first_loc + i: i for i in range(m)},
        compiler_params=params(),
        cost_estimate=cost(1 + len(rounds)),
        name="cross_part",
    )(order, bits, rows, weights, *states, *pres, *c_stacks, *locs, *([] if last else [own]))


def combine(r, bits, own, got, pre):
    right = bits[r] == 1
    own_tot = own[ROWS:]
    got_tot = got[ROWS:]
    scale = jnp.exp(jnp.where(right, own_tot, got_tot))[:HEADS]
    scale = jnp.broadcast_to(scale[:, None], (HEADS, WIDTH, STATE)).reshape(ROWS, STATE)
    scale = jnp.concatenate([scale, jnp.ones((8, STATE), F32)], axis=0)
    new = scale * jnp.where(right, got, own) + jnp.where(right, own, got)
    return new, got[:ROWS].astype(BF16), pre + jnp.where(right, got_tot, 0.0)


def y_shift(x, k):
    return lax.ppermute(x, "head", [(i, ((i // 2 + k) % 4) * 2 + i % 2) for i in range(8)])


def other_core(x):
    return lax.ppermute(x, "head", [(i, i ^ 1) for i in range(8)])


def partner(r, i):
    x, z = i // 8, i % 8
    if r == 0:
        z = z ^ 1
    elif r == 1:
        z = z ^ 2
    elif r == 2:
        z = 7 - z
    elif r == 3:
        x = x ^ 1
    else:
        x = 3 - x
    return x * 8 + z


def exchange(r, x):
    return lax.ppermute(x, "seq", [(i, partner(r, i)) for i in range(32)])


def on_device(values, b_rows, c_rows, log_decay, level_weight):
    me = lax.axis_index("head")
    index = lax.axis_index("seq")
    q = lax.iota(jnp.int32, PIECES)
    far = jnp.where(q < 6, (q >= 3).astype(jnp.int32), q & 1)
    near = q - 3 * far
    turn = jnp.where(q < 6, (4 - near - (near >> 1)) & 3, 2)
    order = ((((me >> 1) - turn) & 3) << 1) | ((me & 1) ^ far)
    bits = (index >> lax.iota(jnp.int32, CROSS)) & 1
    b1, b3, b2 = (y_shift(b_rows, k) for k in (1, 3, 2))
    rows = decay_rows(log_decay)
    (c_own,) = hold([c_rows], [rows])
    near = [*hold([b_rows, b3, b1], [rows, c_own]), b2]
    near_far = [other_core(x) for x in near]
    b_list = near[:3] + near_far[:3] + [near[3], near_far[3]]
    agg_a, top_a = block_states(0, order, values, rows, b_list[:3])
    agg_b, tree, own = block_states(1, order, values, rows, b_list[3:], [top_a])
    c3 = y_shift(c_own, 3)
    (c_late,) = hold([c_own], [own])
    c1 = y_shift(c_late, 1)
    c2 = y_shift(c3, 3)
    c_a = stack([c_own, c3, c1], [])
    c_b = other_core(c_a)
    c_d = other_core(c2)
    c_stacks = [c_a, c_b, c2[None], c_d[None]]
    stacks = ([agg_a, agg_b, agg_b, agg_b], b_list, c_stacks)
    local_args = (order, values, rows, level_weight, tree)
    cross_args = (order, bits, rows, level_weight)
    pre = jnp.zeros((8, STATE), F32)
    pres, states, locs = [], [], []
    for r in range(CROSS):
        sent = own if r < CROSS - 1 else own[:ROWS].astype(BF16)
        got = exchange(r, sent)
        pres.append(pre)
        if r < CROSS - 1 and SHARES[r]:
            loc, own = local_part(SHARES[r], *local_args, own, *stacks)
            locs.append(loc)
        elif r == CROSS - 1:
            locs = cross_part((0, 1, 2, 3), *cross_args, states, pres[:4], c_stacks, locs, sent, False)
            return cross_part((4,), *cross_args, [got], [pre], c_stacks, locs)
        own, st, pre = combine(r, bits, own, got, pre)
        states.append(st)


def solution(mesh):
    return jax.shard_map(
        on_device,
        mesh=mesh,
        in_specs=(
            P("head", None, "seq"),
            P(None, ("seq", "head")),
            P(None, ("seq", "head")),
            P("head", "seq"),
            P(None, "head", "seq"),
        ),
        out_specs=P("head", None, "seq"),
        check_vma=False,
    )
```

```python
import functools

import jax
import jax.numpy as jnp
from jax import lax
from jax.experimental import pallas as pl
from jax.experimental.pallas import tpu as pltpu
from jax.sharding import PartitionSpec as P

STRETCH = 64
HEADS = 3
WIDTH = 64
STATE = 128
ROWS = HEADS * WIDTH
PIECE = 512
PIECES = 8
TOKENS = PIECE * PIECES
LOCAL = 6
CROSS = 5
FIRST = (0, 32, 48, 56, 60, 62, 63)
SHARES = ((), (0, 1, 2), (3, 4, 5), (6, 7))
GROUPS = ((0, 1, 2), (3, 4, 5), (6,), (7,))
STEPS = ((0, 1, 2), (3, 4, 5, 6, 7))
VMEM_LIMIT = 20 * 1024 * 1024
BINV, DEC, GRP = 8, 9, 10
F32 = jnp.float32
BF16 = jnp.bfloat16

VMEM = pl.BlockSpec(memory_space=pltpu.VMEM)
SMEM = pl.BlockSpec(memory_space=pltpu.SMEM)
ANY = pl.BlockSpec(memory_space=pl.ANY)


def params():
    return pltpu.CompilerParams(vmem_limit_bytes=VMEM_LIMIT)


def cost(us):
    return pl.CostEstimate(flops=0, bytes_accessed=int(us * 3_500_000), transcendentals=0)


def decay_kernel(ld_ref, out_ref, run_ref):
    tiles = TOKENS // 128
    batch = 8
    lane = lax.broadcasted_iota(jnp.int32, (HEADS, 128), 1)
    local = lane & 63

    def first(g, carry):
        for i in range(batch):
            cols = pl.ds(pl.multiple_of(g * (batch * 128) + i * 128, 128), 128)
            ld = ld_ref[:, cols]
            cum = ld
            for k in (1, 2, 4, 8, 16, 32):
                cum = cum + jnp.where(local >= k, pltpu.roll(cum, k, 1), 0.0)
            rest = ld
            for k in (1, 2, 4, 8, 16, 32):
                rest = rest + jnp.where(local < 64 - k, pltpu.roll(rest, 128 - k, 1), 0.0)
            grow = jnp.exp(cum)
            out_ref[0, :, cols] = grow
            out_ref[1, :, cols] = jnp.where(lane >= 64, grow, 0.0)
            out_ref[DEC, :, cols] = jnp.exp(rest - ld)
            out_ref[BINV, :, cols] = jnp.exp(-cum)
            out_ref[GRP, :, cols] = jnp.broadcast_to(grow[:, 127:128], (HEADS, 128))
            left = jnp.broadcast_to(cum[:, 63:64], (HEADS, 128))
            run_ref[:, cols] = cum + jnp.where(lane >= 64, left, 0.0)
        return carry

    lax.fori_loop(0, tiles // batch, first, 0)
    runs = [run_ref[:, pl.ds(i * 128, 128)] for i in range(tiles)]
    for level in range(2, LOCAL + 2):
        span = 2 ** (level - 2)
        ends = [jnp.broadcast_to(runs[i][:, 127:128], (HEADS, 128)) for i in range(span - 1, tiles, span)]
        for i in range(tiles):
            cols = pl.ds(i * 128, 128)
            if level > LOCAL or (i // span) % 2:
                out_ref[level, :, cols] = jnp.exp(runs[i])
            else:
                out_ref[level, :, cols] = jnp.zeros((HEADS, 128), F32)
        if level <= LOCAL:
            for i in range(tiles // (2 * span)):
                slot = FIRST[level - 1] - 32 + i
                out_ref[GRP + 1, :, pl.ds(slot * 128, 128)] = jnp.exp(ends[2 * i + 1])
            for i in range(tiles):
                if (i // span) % 2:
                    runs[i] = runs[i] + ends[i // span - 1]
        else:
            out_ref[GRP + 1, :, pl.ds(31 * 128, 128)] = ends[0]


def decay_rows(log_decay):
    return pl.pallas_call(
        decay_kernel,
        out_shape=jax.ShapeDtypeStruct((12, HEADS, TOKENS), F32),
        in_specs=[VMEM],
        out_specs=VMEM,
        scratch_shapes=[pltpu.VMEM(log_decay.shape, F32)],
        compiler_params=params(),
        cost_estimate=cost(2),
        name="decay_rows",
    )(log_decay)


def hold_kernel(n, *refs):
    for x_ref, out_ref in zip(refs[:n], refs[-n:]):
        out_ref[...] = x_ref[...]


def hold(xs, after):
    n = len(xs)
    return pl.pallas_call(
        functools.partial(hold_kernel, n),
        out_shape=[jax.ShapeDtypeStruct(x.shape, x.dtype) for x in xs],
        in_specs=[VMEM] * n + [ANY] * len(after),
        out_specs=[VMEM] * n,
        compiler_params=params(),
        cost_estimate=cost(0.2),
        name="hold",
    )(*xs, *after)


def stack_kernel(p0, p1, p2, *refs):
    out_ref = refs[-1]
    out_ref[0] = p0[...]
    out_ref[1] = p1[...]
    out_ref[2] = p2[...]


def stack(parts, after):
    return pl.pallas_call(
        stack_kernel,
        out_shape=jax.ShapeDtypeStruct((3, STATE, PIECE), BF16),
        in_specs=[VMEM] * 3 + [ANY] * len(after),
        out_specs=VMEM,
        compiler_params=params(),
        cost_estimate=cost(0.2),
        name="stack_pieces",
    )(*parts, *after)


def state_kernel(group, order_ref, v_ref, row_ref, *refs):
    pieces = STEPS[group]
    last = group == len(STEPS) - 1
    b_refs = refs[: len(pieces)]
    if last:
        old_refs = refs[len(pieces) : len(pieces) + group]
        agg_ref, tree_ref, end_ref, p_ref = refs[-4:]
    else:
        agg_ref, top_ref = refs[-2:]
    lane = lax.broadcasted_iota(jnp.int32, (WIDTH, 128), 1)
    first = lane < 64

    def factor(h, slot):
        if isinstance(slot, int):
            return row_ref[GRP + slot // 32, h : h + 1, pl.ds(slot % 32 * 128, 128)]
        return row_ref[GRP + (slot >> 5), h : h + 1, pl.ds(pl.multiple_of((slot & 31) * 128, 128), 128)]

    for q, k in enumerate(pieces):
        j = order_ref[k]
        for h in range(HEADS):
            here = slice(h * WIDTH, (h + 1) * WIDTH)
            tops = []
            for a in range(4):
                cols = pl.ds(pl.multiple_of(j * PIECE + a * 128, 128), 128)
                b = b_refs[q][:, a * 128 : (a + 1) * 128].astype(F32)
                v = v_ref[h, :, cols]
                keys = (row_ref[DEC, h : h + 1, cols] * b).astype(BF16)
                zero = jnp.zeros_like(v)
                both = jnp.concatenate([jnp.where(first, v, zero), jnp.where(first, zero, v)], axis=0)
                s = lax.dot_general(both, keys, (((1,), (1,)), ((), ())), preferred_element_type=F32)
                agg_ref[q, a, here, :] = s[:WIDTH].astype(BF16)
                tops.append(factor(h, j * 4 + a) * s[:WIDTH] + s[WIDTH:])
            agg_ref[q, 4, here, :] = tops[0].astype(BF16)
            agg_ref[q, 5, here, :] = tops[2].astype(BF16)
            lo = factor(h, FIRST[1] + j * 2) * tops[0] + tops[1]
            hi = factor(h, FIRST[1] + j * 2 + 1) * tops[2] + tops[3]
            agg_ref[q, 6, here, :] = lo.astype(BF16)
            top = factor(h, FIRST[2] + j) * lo + hi
            if last:
                p_ref[j, here, :] = top
            else:
                top_ref[q, here, :] = top
    if not last:
        return
    for g, old in enumerate(old_refs):
        for q, k in enumerate(STEPS[g]):
            p_ref[order_ref[k]] = old[q]
    for h in range(HEADS):
        here = slice(h * WIDTH, (h + 1) * WIDTH)
        tops = [p_ref[j, here, :] for j in range(PIECES)]
        for level in range(4, LOCAL + 1):
            nxt = []
            for i in range(len(tops) // 2):
                slot = FIRST[level - 1] + i
                tree_ref[slot - FIRST[3], here, :] = tops[2 * i].astype(BF16)
                nxt.append(factor(h, slot) * tops[2 * i] + tops[2 * i + 1])
            tops = nxt
        end_ref[here, :] = tops[0]
    end_ref[ROWS : ROWS + 8, :] = jnp.concatenate([row_ref[GRP + 1, :, 31 * 128 :], jnp.zeros((5, 128), F32)], axis=0)


def block_states(group, order, values, rows, b_list, old=(), after=()):
    n = len(STEPS[group])
    agg = jax.ShapeDtypeStruct((n, 7, ROWS, STATE), BF16)
    tops = jax.ShapeDtypeStruct((n, ROWS, STATE), F32)
    end = [jax.ShapeDtypeStruct((7, ROWS, STATE), BF16), jax.ShapeDtypeStruct((ROWS + 8, STATE), F32)]
    last = group == len(STEPS) - 1
    return pl.pallas_call(
        functools.partial(state_kernel, group),
        out_shape=[agg] + (end if last else [tops]),
        in_specs=[SMEM] + [VMEM] * (2 + len(b_list) + len(old)) + [ANY] * len(after),
        out_specs=[VMEM] * (3 if last else 2),
        scratch_shapes=[pltpu.VMEM((PIECES, ROWS, STATE), F32)] if last else [],
        compiler_params=params(),
        cost_estimate=cost(1.5),
        name="block_states",
    )(order, values, rows, *b_list, *old, *after)


def home(piece):
    for g, group in enumerate(GROUPS):
        if piece in group:
            return g, group.index(piece)


def local_kernel(pieces, order_ref, v_ref, row_ref, lw_ref, tree_ref, own_ref, *refs):
    out_ref, same_ref = refs[-2:]
    same_ref[...] = own_ref[...]
    used = sorted({home(k)[0] for k in pieces})
    s_id = lax.broadcasted_iota(jnp.int32, (128, 128), 0)
    t_id = lax.broadcasted_iota(jnp.int32, (128, 128), 1)
    keep = (s_id <= t_id) & ((s_id >> 6) == (t_id >> 6))
    for at, k in enumerate(pieces):
        g, q = home(k)
        b_ref = refs[at]
        agg_ref, c_ref = refs[len(pieces) + 2 * used.index(g) :][:2]
        j = order_ref[k]
        for a in range(4):
            cols = pl.ds(pl.multiple_of(j * PIECE + a * 128, 128), 128)
            mine = slice(a * 128, (a + 1) * 128)
            c = c_ref[q, :, mine]
            b = b_ref[:, mine]
            scores = lax.dot_general(b, c, (((0,), (0,)), ((), ())), preferred_element_type=F32)
            scores = jnp.where(keep, scores, 0.0)
            n = k - GROUPS[min(g, 1)][0]
            slots = [(1, agg_ref[n, a])]
            if a & 1:
                slots.append((2, agg_ref[n, 4 + a // 2]))
            if a & 2:
                slots.append((3, agg_ref[n, 6]))
            for level in range(4, LOCAL + 1):
                slots.append((level, tree_ref[FIRST[level - 1] - FIRST[3] + (j >> (level - 3))]))
            every = jnp.dot(jnp.concatenate([x for _, x in slots], axis=0), c, preferred_element_type=F32)
            for h in range(HEADS):
                col = jnp.transpose(jnp.broadcast_to(row_ref[BINV, h : h + 1, cols], (128, 128)))
                mix = ((lw_ref[0, h : h + 1, cols] * row_ref[0, h : h + 1, cols] * scores) * col).astype(BF16)
                acc = jnp.dot(v_ref[h, :, cols], mix, preferred_element_type=F32)
                for i, (level, _) in enumerate(slots):
                    read = every[i * ROWS + h * WIDTH : i * ROWS + (h + 1) * WIDTH]
                    acc = acc + lw_ref[level, h : h + 1, cols] * row_ref[level, h : h + 1, cols] * read
                out_ref[at, h, :, mine] = acc


def local_part(pieces, order, values, rows, weights, tree, own, aggs, b_list, c_stacks):
    used = sorted({home(k)[0] for k in pieces})
    parts = [b_list[k] for k in pieces] + [x[i] for i in used for x in (aggs, c_stacks)]
    return pl.pallas_call(
        functools.partial(local_kernel, pieces),
        out_shape=[
            jax.ShapeDtypeStruct((len(pieces), HEADS, WIDTH, PIECE), F32),
            jax.ShapeDtypeStruct(own.shape, own.dtype),
        ],
        in_specs=[SMEM] + [VMEM] * (5 + len(parts)),
        out_specs=[VMEM] * 2,
        compiler_params=params(),
        cost_estimate=cost(len(pieces)),
        name="local_part",
    )(order, values, rows, weights, tree, own, *parts)


def cross_kernel(rounds, sizes, last, order_ref, bits_ref, row_ref, lw_ref, *refs):
    n, m = len(rounds), len(sizes)
    s_refs, pre_refs = refs[:n], refs[n : 2 * n]
    w = len(GROUPS)
    c_refs = refs[2 * n : 2 * n + w]
    loc_refs = refs[2 * n + w : 2 * n + w + m]
    outs = refs[2 * n + w + m :]
    if last:
        full_ref, stage, sems = outs
    else:
        own_ref, outs, same_ref = outs[0], outs[1 : 1 + m], outs[1 + m :]
        if same_ref:
            same_ref[0][...] = own_ref[...]

    def send(k):
        cols = pl.ds(pl.multiple_of(order_ref[k] * PIECE, PIECE), PIECE)
        return pltpu.make_async_copy(stage.at[k], full_ref.at[:, :, cols], sems.at[k])

    facs = []
    for k, r in enumerate(rounds):
        row = jnp.where(bits_ref[r] == 1, jnp.exp(pre_refs[k][:HEADS, :]), 0.0)
        facs.append(jnp.concatenate([row, row], axis=1))
    states = jnp.concatenate([x[...] for x in s_refs], axis=0)
    place = [(g, o) for g in range(m) for o in range(sizes[g])]
    for q, (g, o) in enumerate(place):
        cg, ci = home(q)
        for a in range(2):
            cols = pl.ds(pl.multiple_of(order_ref[q] * PIECE + a * 256, 256), 256)
            mine = slice(a * 256, (a + 1) * 256)
            every = jnp.dot(states, c_refs[cg][ci, :, mine], preferred_element_type=F32)
            for h in range(HEADS):
                acc = loc_refs[g][o, h, :, mine]
                grow = row_ref[1 + LOCAL, h : h + 1, cols]
                for k, r in enumerate(rounds):
                    row = lw_ref[1 + LOCAL + r, h : h + 1, cols] * grow * facs[k][h : h + 1, :]
                    acc = acc + row * every[k * ROWS + h * WIDTH : k * ROWS + (h + 1) * WIDTH]
                if last:
                    stage[q, h, :, mine] = acc.astype(BF16)
                else:
                    outs[g][o, h, :, mine] = acc
        if last:
            send(q).start()
    if last:
        for q in range(PIECES):
            send(q).wait()


def cross_part(rounds, order, bits, rows, weights, states, pres, c_stacks, locs, own=None, back=True):
    last = own is None
    full = jax.ShapeDtypeStruct((HEADS, WIDTH, TOKENS), BF16)
    same = [jax.ShapeDtypeStruct(x.shape, x.dtype) for x in list(locs) + ([own] if back and not last else [])]
    first_loc = 4 + 2 * len(rounds) + len(GROUPS)
    m = len(locs)
    owns = [] if last else [VMEM if back else ANY]
    return pl.pallas_call(
        functools.partial(cross_kernel, rounds, tuple(x.shape[0] for x in locs), last),
        out_shape=full if last else same,
        in_specs=[SMEM] * 2 + [VMEM] * (2 + 2 * len(rounds) + len(GROUPS) + m) + owns,
        out_specs=ANY if last else [VMEM] * len(same),
        scratch_shapes=[
            pltpu.VMEM((PIECES, HEADS, WIDTH, PIECE), BF16),
            pltpu.SemaphoreType.DMA((PIECES,)),
        ]
        if last
        else [],
        input_output_aliases={} if last else {first_loc + i: i for i in range(m)},
        compiler_params=params(),
        cost_estimate=cost(1 + len(rounds)),
        name="cross_part",
    )(order, bits, rows, weights, *states, *pres, *c_stacks, *locs, *([] if last else [own]))


def combine(r, bits, own, got, pre):
    right = bits[r] == 1
    own_tot = own[ROWS:]
    got_tot = got[ROWS:]
    scale = jnp.exp(jnp.where(right, own_tot, got_tot))[:HEADS]
    scale = jnp.broadcast_to(scale[:, None], (HEADS, WIDTH, STATE)).reshape(ROWS, STATE)
    scale = jnp.concatenate([scale, jnp.ones((8, STATE), F32)], axis=0)
    new = scale * jnp.where(right, got, own) + jnp.where(right, own, got)
    return new, got[:ROWS].astype(BF16), pre + jnp.where(right, got_tot, 0.0)


def y_shift(x, k):
    return lax.ppermute(x, "head", [(i, ((i // 2 + k) % 4) * 2 + i % 2) for i in range(8)])


def other_core(x):
    return lax.ppermute(x, "head", [(i, i ^ 1) for i in range(8)])


def partner(r, i):
    x, z = i // 8, i % 8
    if r == 0:
        z = z ^ 1
    elif r == 1:
        z = z ^ 2
    elif r == 2:
        z = z ^ 6
    elif r == 3:
        x = x ^ 1
    else:
        x = 3 - x
    return x * 8 + z


def exchange(r, x):
    return lax.ppermute(x, "seq", [(i, partner(r, i)) for i in range(32)])


def on_device(values, b_rows, c_rows, log_decay, level_weight):
    me = lax.axis_index("head")
    index = lax.axis_index("seq")
    q = lax.iota(jnp.int32, PIECES)
    far = jnp.where(q < 6, (q >= 3).astype(jnp.int32), q & 1)
    near = q - 3 * far
    turn = jnp.where(q < 6, (4 - near - (near >> 1)) & 3, 2)
    order = ((((me >> 1) - turn) & 3) << 1) | ((me & 1) ^ far)
    bits = (index >> lax.iota(jnp.int32, CROSS)) & 1
    b1, b3, b2 = (y_shift(b_rows, k) for k in (1, 3, 2))
    rows = decay_rows(log_decay)
    (c_own,) = hold([c_rows], [rows])
    near = [*hold([b_rows, b3, b1], [rows, c_own]), b2]
    near_far = [other_core(x) for x in near]
    b_list = near[:3] + near_far[:3] + [near[3], near_far[3]]
    agg_a, top_a = block_states(0, order, values, rows, b_list[:3])
    agg_b, tree, own = block_states(1, order, values, rows, b_list[3:], [top_a])
    c3 = y_shift(c_own, 3)
    (c_late,) = hold([c_own], [own])
    c1 = y_shift(c_late, 1)
    c2 = y_shift(c3, 3)
    c_a = stack([c_own, c3, c1], [])
    c_b = other_core(c_a)
    c_d = other_core(c2)
    c_stacks = [c_a, c_b, c2[None], c_d[None]]
    stacks = ([agg_a, agg_b, agg_b, agg_b], b_list, c_stacks)
    local_args = (order, values, rows, level_weight, tree)
    cross_args = (order, bits, rows, level_weight)
    pre = jnp.zeros((8, STATE), F32)
    pres, states, locs = [], [], []
    for r in range(CROSS):
        sent = own if r < CROSS - 1 else own[:ROWS].astype(BF16)
        got = exchange(r, sent)
        pres.append(pre)
        if r < CROSS - 1 and SHARES[r]:
            loc, own = local_part(SHARES[r], *local_args, own, *stacks)
            locs.append(loc)
        elif r == CROSS - 1:
            locs = cross_part((0, 1, 2, 3), *cross_args, states, pres[:4], c_stacks, locs, sent, False)
            return cross_part((4,), *cross_args, [got], [pre], c_stacks, locs)
        own, st, pre = combine(r, bits, own, got, pre)
        states.append(st)


def solution(mesh):
    return jax.shard_map(
        on_device,
        mesh=mesh,
        in_specs=(
            P("head", None, "seq"),
            P(None, ("seq", "head")),
            P(None, ("seq", "head")),
            P("head", "seq"),
            P(None, "head", "seq"),
        ),
        out_specs=P("head", None, "seq"),
        check_vma=False,
    )
```
